256 devices in a mesh: dp: 32 (over x, z_lo, y), tensor: 8 (over z_hi, core).
Axes of the slice: x: 4, y: 4, z: 8 (z_hi: 4, z_lo: 2; z = z_hi * 2 + z_lo), core: 2. Of those that a mesh axis runs over, the one named last changes fastest.
Arguments:
- tokens: bfloat16 [2560, 2048], P('dp', 'tensor'), may hold values from -6 to 6
- gate_weight: bfloat16 [2048, 8192], P('tensor', 'dp'), may hold values from -0.125 to 0.125
- up_weight: bfloat16 [2048, 8192], P('tensor', 'dp'), may hold values from -0.125 to 0.125
- down_weight: bfloat16 [8192, 2048], P('dp', 'tensor'), may hold values from -0.0625 to 0.0625
- out_grad: bfloat16 [2560, 2048], P('dp', 'tensor'), may hold values from -6 to 6
Outputs:
- mixed: float32 [2560, 2048], P('dp', 'tensor')
- grad_tokens: float32 [2560, 2048], P('dp', 'tensor')
- grad_gate: bfloat16 [2048, 8192], P('tensor', 'dp')
- grad_up: bfloat16 [2048, 8192], P('tensor', 'dp')
- grad_down: bfloat16 [8192, 2048], P('dp', 'tensor')
The draws below stay inside these ranges and needn't reach their ends.
All inputs are finite; a program needn't handle non-finite values.
Results may differ from the reference program's by a relative error of at most 0.0073.
Values may be sent and summed in bfloat16 or wider, within the bound.
A program may use at most 64 MiB of HBM per device.

```python
import math
import jax
import jax.numpy as jnp
from jax import lax

D = 2048
FF = 8192
TOKENS = 2560


def level_of(key, extent, pieces, least, top_value):
    loudness, own = 1.0, jax.random.fold_in(key, 6)
    for dim, blocks in pieces:
        draws = jnp.exp(jax.random.uniform(jax.random.fold_in(own, dim), (blocks,), jnp.float32, least / len(pieces), top_value / len(pieces)))
        loudness = loudness * jnp.repeat(draws, extent[dim] // blocks).reshape([-1 if axis == dim else 1 for axis in range(len(extent))])
    return loudness


def gaussian(key, extent, scale, bound, cuts=(), kind=jnp.bfloat16):
    drawn = scale * jax.random.normal(key, extent, jnp.float32)
    if cuts:
        drawn = drawn * level_of(key, extent, cuts, -0.22, 0.18)
    return jnp.clip(drawn, -bound, bound).astype(kind)


def setup_inputs(seed: int = 0) -> dict:
    seeds = jax.random.split(jax.random.key(seed), 6)
    tokens = gaussian(seeds[0], (TOKENS, D), 1.0, 6.0, ((0, 32), (1, 8)))
    gate_weight = gaussian(seeds[1], (D, FF), D ** -0.5, 0.125, ((0, 8), (1, 32)))
    up_weight = gaussian(seeds[2], (D, FF), D ** -0.5, 0.125, ((0, 8), (1, 32)))
    down_weight = gaussian(seeds[3], (FF, D), FF ** -0.5, 0.0625, ((0, 32), (1, 8)))
    out_grad = gaussian(seeds[4], (TOKENS, D), 1.0, 6.0, ((0, 32), (1, 8)))
    return dict(tokens=tokens, gate_weight=gate_weight, up_weight=up_weight, down_weight=down_weight, out_grad=out_grad)


def sylvester_table(order):
    rows = jnp.arange(order, dtype=jnp.int32)[:, None]
    cols = jnp.arange(order, dtype=jnp.int32)[None, :]
    signs = jnp.ones((order, order), jnp.float32)
    for level in range(order.bit_length() - 1):
        bit_on = jnp.bitwise_and(jnp.bitwise_and(jnp.right_shift(rows, level), jnp.right_shift(cols, level)), 1)
        signs = signs * (1.0 - 2.0 * bit_on.astype(jnp.float32))
    return signs

def rotate_rows(values):
    count = values.shape[0]
    lanes = min(D, 128)
    blocks = D // lanes
    shaped = values.reshape(count, blocks, lanes)
    shaped = jnp.einsum('rab,ac->rcb', shaped, sylvester_table(blocks), precision=lax.Precision.HIGHEST)
    shaped = jnp.einsum('rcb,bd->rcd', shaped, sylvester_table(lanes), precision=lax.Precision.HIGHEST)
    return shaped.reshape(count, D) * (1.0 / math.sqrt(D))

def reference(tokens, gate_weight, up_weight, down_weight, out_grad):
    rotated = rotate_rows(tokens.astype(jnp.float32)).astype(jnp.bfloat16)
    gate = jnp.dot(rotated, gate_weight, preferred_element_type=jnp.float32)
    up = jnp.dot(rotated, up_weight, preferred_element_type=jnp.float32)
    hidden = (jax.nn.silu(gate) * up).astype(jnp.bfloat16)
    mixed = rotate_rows(jnp.dot(hidden, down_weight, preferred_element_type=jnp.float32))
    grad_rot = rotate_rows(out_grad.astype(jnp.float32)).astype(jnp.bfloat16)
    grad_hidden = jnp.dot(grad_rot, down_weight.T, preferred_element_type=jnp.float32)
    sigma = jax.nn.sigmoid(gate)
    grad_gate_act = (grad_hidden * up * sigma * (1.0 + gate * (1.0 - sigma))).astype(jnp.bfloat16)
    grad_up_act = (grad_hidden * gate * sigma).astype(jnp.bfloat16)
    summed = jnp.dot(grad_gate_act, gate_weight.T, preferred_element_type=jnp.float32)
    summed = summed + jnp.dot(grad_up_act, up_weight.T, preferred_element_type=jnp.float32)
    grad_tokens = rotate_rows(summed)
    factor = 1.0 / math.sqrt(TOKENS)
    grad_gate = (jnp.dot(rotated.T, grad_gate_act, preferred_element_type=jnp.float32) * factor).astype(jnp.bfloat16)
    grad_up = (jnp.dot(rotated.T, grad_up_act, preferred_element_type=jnp.float32) * factor).astype(jnp.bfloat16)
    grad_down = (jnp.dot(hidden.T, grad_rot, preferred_element_type=jnp.float32) * factor).astype(jnp.bfloat16)
    return (mixed, grad_tokens, grad_gate, grad_up, grad_down)
```

```python
import math

import jax
import jax.numpy as jnp
from jax import lax
from jax.experimental import pallas as pl
from jax.experimental.pallas import tpu as pltpu
from jax.sharding import PartitionSpec as P

D = 2048
TOKENS = 2560
ROWS = 80
LANES = 256
UNITS = 64
MESH = pl.DeviceIdType.MESH
F32 = jnp.float32
BF16 = jnp.bfloat16


def dot_nn(a, b):
    return lax.dot_general(a, b, (((1,), (0,)), ((), ())), preferred_element_type=F32)


def dot_nt(a, b):
    return lax.dot_general(a, b, (((1,), (1,)), ((), ())), preferred_element_type=F32)


def butterflies(parts):
    parts = list(parts)
    for bit in range(3):
        step = 1 << bit
        for low in range(8):
            if not low & step:
                a, b = parts[low], parts[low | step]
                parts[low], parts[low | step] = a + b, a - b
    return parts


def kernel(tok, og, gw, uw, dw, mixed, gtok, gg, gu, gd,
           AB, PK, WB, H, FS, ROT, HID, GACT, MP, R1, R2, ZS, ZR,
           WO, CS, CR, XS, X1, X2, ZW, ZWR, GTT,
           zs, zr, ws, wr, ys, yr, y2s, y2r, xs, xr, x2s, x2r, cs, cr, os_, or_, os2, or2,
           es, er, gs, gr, vs, vr):
    dp = lax.axis_index("dp")
    te = lax.axis_index("tensor")
    x, zl, y = dp // 8, (dp // 4) % 2, dp % 4
    zh, c = te // 2, te % 2
    z = 2 * zh + zl
    k_own = te
    other = 1 - c
    home = c == zl
    xp, xm, xf = (x + 1) % 4, (x + 3) % 4, (x + 2) % 4
    yp, ym, yf = (y + 1) % 4, (y + 3) % 4, (y + 2) % 4

    def did(x_, y_, z_, c_):
        return ((x_ * 2 + z_ % 2) * 4 + y_, (z_ // 2) * 2 + c_)

    def rc(src, dst, send, recv, dev):
        return pltpu.make_async_remote_copy(
            src_ref=src, dst_ref=dst, send_sem=send, recv_sem=recv,
            device_id=dev, device_id_type=MESH)

    here = did(x, y, z, other)
    dev_x = (did(xp, y, z, c), did(xm, y, z, c))
    dev_y = (did(x, yp, z, c), did(x, ym, z, c))
    sent = []

    def start(src, dst, send, recv, dev):
        cp = rc(src, dst, send, recv, dev)
        cp.start()
        sent.append(cp)

    def arrive(dst, recv):
        rc(dst, dst, recv, recv, here).wait_recv()

    barrier = pltpu.get_barrier_semaphore()

    def greet(dev):
        pl.semaphore_signal(barrier, inc=1, device_id=dev, device_id_type=MESH)

    for dz in range(8):
        for cc in range(2):
            if dz or cc:
                greet(did(x, y, (z + dz) % 8, (c + cc) % 2))
    for dev in dev_x + dev_y:
        greet(dev)

    gwt = gw[...].astype(F32).T.astype(BF16)
    uwt = uw[...].astype(F32).T.astype(BF16)
    for q in range(4):
        PK[q, 0:UNITS] = gwt[q * UNITS:(q + 1) * UNITS]
        PK[q, UNITS:2 * UNITS] = uwt[q * UNITS:(q + 1) * UNITS]
        PK[q, 2 * UNITS:3 * UNITS] = dw[q * UNITS:(q + 1) * UNITS, :]
    i = lax.broadcasted_iota(jnp.int32, (LANES, LANES), 0)
    j = lax.broadcasted_iota(jnp.int32, (LANES, LANES), 1)
    b = i & j
    b = b ^ (b >> 4)
    b = b ^ (b >> 2)
    b = (b ^ (b >> 1)) & 1
    H[...] = (1 - 2 * b).astype(F32).astype(BF16)
    WB[x, c, zh] = PK[zh]

    pl.semaphore_wait(barrier, 19)

    def send_tokens(a, ref):
        for dz in (1, 7, 0, 2, 6, 3, 5, 4):
            cp = rc(ref, AB.at[a, y, k_own], zs.at[a, dz], zr.at[a, k_own],
                    did(x, y, (z + dz) % 8, zl))
            if dz:
                cp.start()
                sent.append(cp)
            else:
                @pl.when(home)
                def _():
                    AB[a, y, k_own] = ref[...]

                @pl.when(jnp.logical_not(home))
                def _():
                    cp.start()

    def send_weights():
        for q in (1, 3, 2):
            to = (zh + q) % 4
            start(PK.at[to], WB.at[x, c, zh], ws.at[q], wr.at[q], did(x, y, 2 * to + zl, c))

    send_tokens(0, tok)
    send_weights()
    send_tokens(1, og)

    order = (0, 1, 3, 2)

    def pair(a, yy, pos):
        return AB.at[a, yy, pl.ds(2 * ((zh + order[pos]) % 4), 2)]

    def tokens_z(a):
        for pos in range(4):
            from_zh = (zh + order[pos]) % 4
            k_same, k_other = 2 * from_zh + c, 2 * from_zh + other
            arrive(AB.at[a, y, k_other], zr.at[a, k_other])
            if pos == 0:
                @pl.when(jnp.logical_not(home))
                def _():
                    arrive(AB.at[a, y, k_same], zr.at[a, k_same])
            else:
                arrive(AB.at[a, y, k_same], zr.at[a, k_same])
            for way in range(2):
                start(pair(a, y, pos), pair(a, y, pos), ys.at[a, pos, way], yr.at[a, pos, way], dev_y[way])

    def weights_z():
        for q in (0, 1, 3, 2):
            frm = (zh + 4 - q) % 4
            if q:
                arrive(WB.at[x, c, frm], wr.at[q])
            for way in range(2):
                start(WB.at[x, c, frm], WB.at[x, c, frm], xs.at[q, way], xr.at[q, way], dev_x[way])
        start(WB.at[x, c], WB.at[x, c], cs.at[0], cr.at[0], here)

    def tokens_y(a):
        for pos in range(4):
            for way in range(2):
                frm = (ym, yp)[way]
                arrive(pair(a, frm, pos), yr.at[a, pos, way])
                if (pos < 2) == (way == 0):
                    start(pair(a, frm, pos), pair(a, frm, pos), y2s.at[a, pos], y2r.at[a, pos], dev_y[way])

    def weights_x():
        for way in range(2):
            frm = (xm, xp)[way]
            for q in (0, 1, 3, 2):
                arrive(WB.at[frm, c, (zh + 4 - q) % 4], xr.at[q, way])
            half = WB.at[frm, c, pl.ds(2 * way, 2)]
            start(half, half, x2s.at[way], x2r.at[way], dev_x[way])
            start(WB.at[frm, c], WB.at[frm, c], cs.at[1 + way], cr.at[1 + way], here)

    def weights_far():
        for way in range(2):
            arrive(WB.at[xf, c, pl.ds(2 * way, 2)], x2r.at[way])
        start(WB.at[xf, c], WB.at[xf, c], cs.at[3], cr.at[3], here)
        for n, frm in enumerate((x, xm, xp, xf)):
            arrive(WB.at[frm, other], cr.at[n])

    scale = 1.0 / math.sqrt(D)

    def spread(a, yy):
        def step(r, _):
            rows = pl.ds(pl.multiple_of(r * 16, 16), 16)
            parts = butterflies([FS[k, rows] for k in range(8)])
            for k in range(8):
                ROT[a, k, yy, rows] = (parts[k] * scale).astype(BF16)
            return 0
        lax.fori_loop(0, ROWS // 16, step, 0)

    def rotate_in(a, yy):
        FS[...] = dot_nn(AB[a, yy].reshape(8 * ROWS, LANES), H[...]).reshape(8, ROWS, LANES)
        spread(a, yy)

    def tokens_far(a):
        for pos in range(4):
            arrive(pair(a, yf, pos), y2r.at[a, pos])
        rotate_in(a, yf)

    tokens_z(0)
    weights_z()
    tokens_z(1)
    rotate_in(0, y)
    tokens_y(0)
    rotate_in(0, ym)
    rotate_in(0, yp)
    weights_x()
    tokens_y(1)
    rotate_in(1, y)
    rotate_in(1, ym)
    rotate_in(1, yp)
    tokens_far(0)
    weights_far()

    def rot(a, k):
        return ROT[a, k].reshape(4 * ROWS, LANES)

    def weight(w, k):
        return jnp.concatenate(
            [WB[q, k % 2, k // 2, w * UNITS:(w + 1) * UNITS] for q in range(4)], axis=0)

    rot_tok = jnp.concatenate([rot(0, k) for k in range(8)], axis=1)

    def all_weight(w):
        return jnp.concatenate([weight(w, k) for k in range(8)], axis=1)

    gate = dot_nt(rot_tok, all_weight(0))
    up = dot_nt(rot_tok, all_weight(1))
    sigma = 1.0 / (1.0 + jnp.exp(-gate))
    hidden = (gate * sigma * up).astype(BF16)
    HID[...] = hidden
    GACT[0] = up * sigma * (1.0 + gate * (1.0 - sigma))
    GACT[1] = gate * sigma

    def halves(a):
        lo, hi = pl.ds(0, 4), pl.ds(4, 4)
        start(MP.at[a, yf, lo], R1.at[a, 0], os_.at[a, 0], or_.at[a, 0], dev_y[0])
        start(MP.at[a, yf, hi], R1.at[a, 1], os_.at[a, 1], or_.at[a, 1], dev_y[1])
        start(MP.at[a, yp, hi], R2.at[a, 0, hi], os_.at[a, 2], or_.at[a, 2], dev_y[0])
        start(MP.at[a, ym, lo], R2.at[a, 1, lo], os_.at[a, 3], or_.at[a, 3], dev_y[1])

    def pass_on(a):
        lo, hi = pl.ds(0, 4), pl.ds(4, 4)
        arrive(R1.at[a, 0], or_.at[a, 0])
        MP[a, yp, 0:4] = (MP[a, yp, 0:4].astype(F32) + R1[a, 0].astype(F32)).astype(BF16)
        start(MP.at[a, yp, lo], R2.at[a, 0, lo], os2.at[a, 0], or2.at[a, 0], dev_y[0])
        arrive(R1.at[a, 1], or_.at[a, 1])
        MP[a, ym, 4:8] = (MP[a, ym, 4:8].astype(F32) + R1[a, 1].astype(F32)).astype(BF16)
        start(MP.at[a, ym, hi], R2.at[a, 1, hi], os2.at[a, 1], or2.at[a, 1], dev_y[1])

    def rotate_out(a):
        lo, hi = pl.ds(0, 4), pl.ds(4, 4)
        arrive(R2.at[a, 0, hi], or_.at[a, 2])
        arrive(R2.at[a, 1, lo], or_.at[a, 3])
        arrive(R2.at[a, 0, lo], or2.at[a, 0])
        arrive(R2.at[a, 1, hi], or2.at[a, 1])
        total = MP[a, y].astype(F32) + R2[a, 0].astype(F32) + R2[a, 1].astype(F32)
        total = total.reshape(8 * ROWS, LANES)
        high = total.astype(BF16)
        low = (total - high.astype(F32)).astype(BF16)
        FS[...] = (dot_nn(high, H[...]) + dot_nn(low, H[...])).reshape(8, ROWS, LANES)

        def step(r, _):
            rows = pl.ds(pl.multiple_of(r * 16, 16), 16)
            parts = butterflies([FS[k, rows] for k in range(8)])
            for k in range(8):
                ZS[a, k, rows] = (parts[k] * scale).astype(BF16)
            return 0
        lax.fori_loop(0, ROWS // 16, step, 0)
        for q in (0, 1, 3, 2):
            to = (zh + q) % 4
            for cc in (0, 1):
                to_c = (c + cc) % 2
                src = ZS.at[a, 2 * to + to_c]
                cp = rc(src, ZR.at[a, z], es.at[a, 2 * q + cc], er.at[a, z], did(x, y, 2 * to + c, to_c))
                if q or cc:
                    cp.start()
                    sent.append(cp)
                else:
                    @pl.when(home)
                    def _():
                        ZR[a, z] = ZS[a, 2 * zh + c]

                    @pl.when(jnp.logical_not(home))
                    def _():
                        cp.start()

    def finish_tokens(a, out):
        for dz in range(8):
            frm = (z + dz) % 8
            if dz:
                arrive(ZR.at[a, frm], er.at[a, frm])
            else:
                @pl.when(jnp.logical_not(home))
                def _():
                    arrive(ZR.at[a, frm], er.at[a, frm])
        total = ZR[a, 0].astype(F32)
        for s in range(1, 8):
            total = total + ZR[a, s].astype(F32)
        out[...] = total

    for k in range(8):
        MP[0, :, k] = dot_nn(hidden, weight(2, k)).astype(BF16).reshape(4, ROWS, LANES)
    halves(0)
    tokens_far(1)
    pass_on(0)

    rot_grad = jnp.concatenate([rot(1, k) for k in range(8)], axis=1)
    grad_hidden = dot_nt(rot_grad, all_weight(2))
    gga = grad_hidden * GACT[0]
    gua = grad_hidden * GACT[1]
    gga_b = gga.astype(BF16)
    gua_b = gua.astype(BF16)
    GTT[0] = gga.T.astype(BF16)
    GTT[1] = gua.T.astype(BF16)
    GTT[2] = HID[...].astype(F32).T.astype(BF16)
    for k in range(8):
        MP[1, :, k] = (dot_nn(gga_b, weight(0, k)) + dot_nn(gua_b, weight(1, k))).astype(BF16).reshape(4, ROWS, LANES)
    halves(1)

    def weight_grads(parity, store):
        def step(q, _):
            k = 2 * q + parity
            for w in range(3):
                g = dot_nn(GTT[w], ROT[w // 2, k].reshape(4 * ROWS, LANES))
                for p in range(4):
                    store(p, q, w, g[p * UNITS:(p + 1) * UNITS])
            return 0
        lax.fori_loop(0, 4, step, 0)

    def store_other(p, q, w, g):
        CS[p, q, w * UNITS:(w + 1) * UNITS] = g.astype(BF16)

    def store_own(p, q, w, g):
        WO[p, q, w * UNITS:(w + 1) * UNITS] = g

    weight_grads(other, store_other)
    for n, p in enumerate((xf, xp, xm, x)):
        start(CS.at[p], CR.at[p], cs.at[4 + n], cr.at[4 + n], here)
    pass_on(1)
    weight_grads(c, store_own)

    arrive(CR.at[xf], cr.at[4])
    XS[xf] = (WO[xf] + CR[xf].astype(F32)).astype(BF16)
    lo, hi = pl.ds(0, 2), pl.ds(2, 2)
    start(XS.at[xf, lo], X1.at[0], gs.at[0], gr.at[0], dev_x[0])
    start(XS.at[xf, hi], X1.at[1], gs.at[1], gr.at[1], dev_x[1])
    arrive(CR.at[xp], cr.at[5])
    XS[xp, 2:4] = (WO[xp, 2:4] + CR[xp, 2:4].astype(F32)).astype(BF16)
    start(XS.at[xp, hi], X2.at[0, hi], gs.at[2], gr.at[2], dev_x[0])
    arrive(CR.at[xm], cr.at[6])
    XS[xm, 0:2] = (WO[xm, 0:2] + CR[xm, 0:2].astype(F32)).astype(BF16)
    start(XS.at[xm, lo], X2.at[1, lo], gs.at[3], gr.at[3], dev_x[1])

    rotate_out(0)

    arrive(X1.at[0], gr.at[0])
    XS[xp, 0:2] = (WO[xp, 0:2] + CR[xp, 0:2].astype(F32) + X1[0].astype(F32)).astype(BF16)
    start(XS.at[xp, lo], X2.at[0, lo], gs.at[4], gr.at[4], dev_x[0])
    arrive(X1.at[1], gr.at[1])
    XS[xm, 2:4] = (WO[xm, 2:4] + CR[xm, 2:4].astype(F32) + X1[1].astype(F32)).astype(BF16)
    start(XS.at[xm, hi], X2.at[1, hi], gs.at[5], gr.at[5], dev_x[1])
    arrive(CR.at[x], cr.at[7])

    rotate_out(1)
    finish_tokens(0, mixed)

    arrive(X2.at[0, hi], gr.at[2])
    arrive(X2.at[1, lo], gr.at[3])
    arrive(X2.at[0, lo], gr.at[4])
    arrive(X2.at[1, hi], gr.at[5])
    factor = 1.0 / math.sqrt(TOKENS)
    for q in range(4):
        total = WO[x, q] + CR[x, q].astype(F32) + X2[0, q].astype(F32) + X2[1, q].astype(F32)
        ZW[q] = (total * factor).astype(BF16)
    for q in (1, 3, 2):
        to = (zh + q) % 4
        start(ZW.at[to], ZWR.at[zh], vs.at[q], vr.at[q], did(x, y, 2 * to + zl, c))
    ZWR[zh] = ZW[zh]

    finish_tokens(1, gtok)

    for q in (1, 3, 2):
        arrive(ZWR.at[(zh + 4 - q) % 4], vr.at[q])
    for w, out in ((0, gg), (1, gu)):
        rows = jnp.concatenate([ZWR[q, w * UNITS:(w + 1) * UNITS] for q in range(4)], axis=0)
        out[...] = rows.astype(F32).T.astype(BF16)
    for q in range(4):
        gd[q * UNITS:(q + 1) * UNITS, :] = ZWR[q, 2 * UNITS:3 * UNITS]

    for cp in sent:
        cp.wait_send()

    @pl.when(jnp.logical_not(home))
    def _():
        for a, ref in ((0, tok), (1, og)):
            rc(ref, AB.at[a, y, k_own], zs.at[a, 0], zr.at[a, k_own], here).wait_send()
            rc(ZS.at[a, 0], ZR.at[a, z], es.at[a, 0], er.at[a, z], here).wait_send()


def shards(tokens, gate_weight, up_weight, down_weight, out_grad):
    dma = pltpu.SemaphoreType.DMA
    vm = pltpu.VMEM
    block = jax.ShapeDtypeStruct
    rows, cols = tokens.shape
    return pl.pallas_call(
        kernel,
        out_shape=(
            block((ROWS, LANES), F32), block((ROWS, LANES), F32),
            block((256, 256), BF16), block((256, 256), BF16), block((256, 256), BF16)),
        in_specs=[pl.BlockSpec(memory_space=vm)] * 5,
        out_specs=[pl.BlockSpec(memory_space=vm)] * 5,
        scratch_shapes=[
            vm((2, 4, 8, ROWS, LANES), BF16),
            vm((4, 192, LANES), BF16),
            vm((4, 2, 4, 192, LANES), BF16),
            vm((LANES, LANES), BF16),
            vm((8, ROWS, LANES), F32),
            vm((2, 8, 4, ROWS, LANES), BF16),
            vm((4 * ROWS, 256), BF16),
            vm((2, 4 * ROWS, 256), F32),
            vm((2, 4, 8, ROWS, LANES), BF16),
            vm((2, 2, 4, ROWS, LANES), BF16),
            vm((2, 2, 8, ROWS, LANES), BF16),
            vm((2, 8, ROWS, LANES), BF16),
            vm((2, 8, ROWS, LANES), BF16),
            vm((4, 4, 192, LANES), F32),
            vm((4, 4, 192, LANES), BF16),
            vm((4, 4, 192, LANES), BF16),
            vm((4, 4, 192, LANES), BF16),
            vm((2, 2, 192, LANES), BF16),
            vm((2, 4, 192, LANES), BF16),
            vm((4, 192, LANES), BF16),
            vm((4, 192, LANES), BF16),
            vm((3, 256, 4 * ROWS), BF16),
            dma((2, 8)), dma((2, 8)), dma((4,)), dma((4,)),
            dma((2, 4, 2)), dma((2, 4, 2)), dma((2, 4)), dma((2, 4)),
            dma((4, 2)), dma((4, 2)), dma((2,)), dma((2,)),
            dma((8,)), dma((8,)), dma((2, 4)), dma((2, 4)), dma((2, 2)), dma((2, 2)),
            dma((2, 8)), dma((2, 8)), dma((6,)), dma((6,)), dma((4,)), dma((4,)),
        ],
        compiler_params=pltpu.CompilerParams(
            collective_id=0, has_side_effects=True, vmem_limit_bytes=48 << 20),
        name="layer",
    )(tokens, out_grad, gate_weight, up_weight, down_weight)


def solution(mesh):
    return jax.shard_map(
        shards,
        mesh=mesh,
        in_specs=(P("dp", "tensor"), P("tensor", "dp"), P("tensor", "dp"), P("dp", "tensor"), P("dp", "tensor")),
        out_specs=(P("dp", "tensor"), P("dp", "tensor"), P("tensor", "dp"), P("tensor", "dp"), P("dp", "tensor")),
        check_vma=False,
    )
```

```python
import math

import jax
import jax.numpy as jnp
from jax import lax
from jax.experimental import pallas as pl
from jax.experimental.pallas import tpu as pltpu
from jax.sharding import PartitionSpec as P

D = 2048
TOKENS = 2560
ROWS = 80
LANES = 256
UNITS = 64
MESH = pl.DeviceIdType.MESH
F32 = jnp.float32
BF16 = jnp.bfloat16


def dot_nn(a, b):
    return lax.dot_general(a, b, (((1,), (0,)), ((), ())), preferred_element_type=F32)


def dot_nt(a, b):
    return lax.dot_general(a, b, (((1,), (1,)), ((), ())), preferred_element_type=F32)


def butterflies(parts):
    parts = list(parts)
    for bit in range(3):
        step = 1 << bit
        for low in range(8):
            if not low & step:
                a, b = parts[low], parts[low | step]
                parts[low], parts[low | step] = a + b, a - b
    return parts


def kernel(tok_hbm, og_hbm, gw, uw, dw, mixed, gtok, gg, gu, gd,
           WIN, TIN, AB, PK, WB, H, FS, WR, ROT, GACT, MP, R1, R2, ZS, ZR,
           WO, CS, CR, XS, X1, X2, ZW, ZWR, GTT,
           loads, zs, zr, zfs, zfr, zes, zer, ws, wr, ys, yr, y2s, y2r, xs, xr, cs, cr, os_, or_, os2, or2,
           es, er, gs, gr, vs, vr):
    dp = lax.axis_index("dp")
    te = lax.axis_index("tensor")
    x, zl, y = dp // 8, (dp // 4) % 2, dp % 4
    zh, c = te // 2, te % 2
    z = 2 * zh + zl
    k_own = te
    other = 1 - c
    home = c == zl
    xp, xm, xf = (x + 1) % 4, (x + 3) % 4, (x + 2) % 4
    yp, ym, yf = (y + 1) % 4, (y + 3) % 4, (y + 2) % 4

    def did(x_, y_, z_, c_):
        return ((x_ * 2 + z_ % 2) * 4 + y_, (z_ // 2) * 2 + c_)

    def rc(src, dst, send, recv, dev):
        return pltpu.make_async_remote_copy(
            src_ref=src, dst_ref=dst, send_sem=send, recv_sem=recv,
            device_id=dev, device_id_type=MESH)

    here = did(x, y, z, other)
    dev_x = (did(xp, y, z, c), did(xm, y, z, c), did(xf, y, z, c))
    dev_y = (did(x, yp, z, c), did(x, ym, z, c))
    sent, sent_home, sent_away = [], [], []

    def start(src, dst, send, recv, dev):
        cp = rc(src, dst, send, recv, dev)
        cp.start()
        sent.append(cp)

    def arrive(dst, recv):
        rc(dst, dst, recv, recv, here).wait_recv()

    barrier = pltpu.get_barrier_semaphore()

    def greet(dev):
        pl.semaphore_signal(barrier, inc=1, device_id=dev, device_id_type=MESH)

    for dz in range(8):
        for cc in range(2):
            if dz or cc:
                greet(did(x, y, (z + dz) % 8, (c + cc) % 2))
    for dev in dev_x + dev_y:
        greet(dev)

    fetched = [pltpu.make_async_copy(ref, WIN.at[n], loads.at[n]) for n, ref in enumerate((gw, uw, dw))]
    fetched_tokens = [pltpu.make_async_copy(ref, TIN.at[n], loads.at[3 + n]) for n, ref in enumerate((tok_hbm, og_hbm))]
    for cp in fetched_tokens + fetched:
        cp.start()
    tok, og = TIN.at[0], TIN.at[1]

    i = lax.broadcasted_iota(jnp.int32, (LANES, LANES), 0)
    j = lax.broadcasted_iota(jnp.int32, (LANES, LANES), 1)
    b = i & j
    b = b ^ (b >> 4)
    b = b ^ (b >> 2)
    b = (b ^ (b >> 1)) & 1
    H[...] = (1 - 2 * b).astype(F32).astype(BF16)

    for cp in fetched:
        cp.wait()
    gwt = WIN[0].astype(F32).T.astype(BF16)
    uwt = WIN[1].astype(F32).T.astype(BF16)
    for q in range(4):
        PK[q, 0:UNITS] = gwt[q * UNITS:(q + 1) * UNITS]
        PK[q, UNITS:2 * UNITS] = uwt[q * UNITS:(q + 1) * UNITS]
        PK[q, 2 * UNITS:3 * UNITS] = WIN[2, q * UNITS:(q + 1) * UNITS, :]
    WB[x, c, zh] = PK[zh]

    for cp in fetched_tokens:
        cp.wait()
    pl.semaphore_wait(barrier, 20)

    dev_z = (did(x, y, (z + 1) % 8, c), did(x, y, (z + 7) % 8, c))
    own_z = (did(x, y, (z + 1) % 8, zl), did(x, y, (z + 7) % 8, zl))
    away = jnp.logical_not(home)

    def send_tokens(a, ref):
        for way in range(2):
            start(ref, AB.at[a, y, k_own], zs.at[a, way], zr.at[a, k_own], own_z[way])

        cp = rc(ref, AB.at[a, y, k_own], zs.at[a, 2], zr.at[a, k_own], here)

        @pl.when(home)
        def _():
            pltpu.make_async_copy(ref, AB.at[a, y, k_own], zs.at[a, 2]).start()

        @pl.when(away)
        def _():
            cp.start()
        sent_away.append(cp)

    def send_weights(q):
        to = (zh + q) % 4
        start(PK.at[to], WB.at[x, c, zh], ws.at[q], wr.at[q], did(x, y, 2 * to + zl, c))

    shift = zl
    at_home = [zh, (zh + 3) % 4, (zh + 1) % 4, (zh + 2) % 4]
    at_away = [(zh + 3 + shift) % 4, (zh + shift) % 4, (zh + 2 + shift) % 4, (zh + 1 + shift) % 4]
    step_zh = [jnp.where(home, p, q) for p, q in zip(at_home, at_away)]

    def pair(a, yy, pos):
        return AB.at[a, yy, pl.ds(2 * step_zh[pos], 2)]

    def tokens_z(a, pos):
        near = step_zh[pos]
        one = [AB.at[a, y, 2 * near + n] for n in range(2)]
        both = pair(a, y, pos)
        sem = [zr.at[a, 2 * near + n] for n in range(2)]

        def relay(way):
            return rc(both, both, zfs.at[a, way], zfr.at[a, near], dev_z[way])

        def last(way):
            return rc(one[way], one[way], zes.at[a, way], zer.at[a, way], dev_z[way])

        if 0 < pos < 3:
            from_home = relay(pos - 1)
            sent_home.append(from_home)
        from_away = relay(pos) if pos < 2 else last(pos - 2)
        sent_away.append(from_away)

        @pl.when(home)
        def _():
            if pos == 0:
                arrive(AB.at[a, y, 2 * near + other], zr.at[a, 2 * near + other])
                pltpu.make_async_copy((tok, og)[a], AB.at[a, y, k_own], zs.at[a, 2]).wait()
            elif pos < 3:
                arrive(both, zfr.at[a, near])
                from_home.start()
            else:
                arrive(one[0], zer.at[a, 0])
                arrive(one[1], zer.at[a, 1])

        @pl.when(away)
        def _():
            if pos < 2:
                arrive(one[0], sem[0])
                arrive(one[1], sem[1])
                from_away.start()
            else:
                arrive(both, zfr.at[a, near])
                from_away.start()

    def tokens_out(a, pos):
        for way in range(2):
            start(pair(a, y, pos), pair(a, y, pos), ys.at[a, pos, way], yr.at[a, pos, way], dev_y[way])

    def weights_z(q):
        frm = (zh + 4 - q) % 4
        if q:
            arrive(WB.at[x, c, frm], wr.at[q])
        for way in range(3):
            start(WB.at[x, c, frm], WB.at[x, c, frm], xs.at[q, way], xr.at[q, way], dev_x[way])

    def tokens_y(a):
        for pos in range(4):
            for way in range(2):
                frm = (ym, yp)[way]
                arrive(pair(a, frm, pos), yr.at[a, pos, way])
                if (pos < 2) == (way == 0):
                    start(pair(a, frm, pos), pair(a, frm, pos), y2s.at[a, pos], y2r.at[a, pos], dev_y[way])

    def weights_x():
        start(WB.at[x, c], WB.at[x, c], cs.at[0], cr.at[0], here)
        for way in range(3):
            frm = (xm, xp, xf)[way]
            for q in (0, 1, 3, 2):
                arrive(WB.at[frm, c, (zh + 4 - q) % 4], xr.at[q, way])
            start(WB.at[frm, c], WB.at[frm, c], cs.at[1 + way], cr.at[1 + way], here)

    def weights_far():
        for n, frm in enumerate((x, xm, xp, xf)):
            arrive(WB.at[frm, other], cr.at[n])

    scale = 1.0 / math.sqrt(D)

    def spread(a, yy):
        def step(r, _):
            rows = pl.ds(pl.multiple_of(r * 16, 16), 16)
            parts = butterflies([FS[k, rows] for k in range(8)])
            for k in range(8):
                ROT[a, k, yy, rows] = (parts[k] * scale).astype(BF16)
            return 0
        lax.fori_loop(0, ROWS // 16, step, 0)

    def rotate_in(a, yy):
        FS[:, 0:ROWS] = dot_nn(AB[a, yy].reshape(8 * ROWS, LANES), H[...]).reshape(8, ROWS, LANES)
        spread(a, yy)

    def tokens_far(a):
        for pos in range(4):
            arrive(pair(a, yf, pos), y2r.at[a, pos])
        rotate_in(a, yf)

    send_tokens(0, tok)
    send_tokens(1, og)
    send_weights(1)
    send_weights(3)
    weights_z(0)
    for pos in range(2):
        for a in range(2):
            tokens_z(a, pos)
            tokens_out(a, pos)
    send_weights(2)
    weights_z(1)
    weights_z(3)
    for pos in range(2, 4):
        for a in range(2):
            tokens_z(a, pos)
            tokens_out(a, pos)
    weights_z(2)
    tokens_y(0)
    rotate_in(0, y)
    rotate_in(0, ym)
    tokens_y(1)
    rotate_in(0, yp)
    weights_x()
    tokens_far(0)
    weights_far()

    def rot(a, k):
        return ROT[a, k].reshape(4 * ROWS, LANES)

    def weight(w, k):
        return jnp.concatenate(
            [WB[q, k % 2, k // 2, w * UNITS:(w + 1) * UNITS] for q in range(4)], axis=0)

    def rotate_weight(w):
        for k in range(8):
            FS[k] = dot_nn(weight(w, k), H[...])

        def step(r, _):
            rows = pl.ds(pl.multiple_of(r * 16, 16), 16)
            parts = butterflies([FS[k, rows] for k in range(8)])
            for k in range(8):
                WR[w, k, rows] = (parts[k] * scale).astype(BF16)
            return 0
        lax.fori_loop(0, 256 // 16, step, 0)

    rot_tok = jnp.concatenate([rot(0, k) for k in range(8)], axis=1)

    def all_weight(w):
        return jnp.concatenate([weight(w, k) for k in range(8)], axis=1)

    gate = dot_nt(rot_tok, all_weight(0))
    up = dot_nt(rot_tok, all_weight(1))
    sigma = 1.0 / (1.0 + jnp.exp(-gate))
    hidden = (gate * sigma * up).astype(BF16)
    GTT[2] = hidden.astype(F32).T.astype(BF16)
    GACT[0] = up * sigma * (1.0 + gate * (1.0 - sigma))
    GACT[1] = gate * sigma

    def chunk(ref, n):
        return ref.at[pl.ds(2 * ((zh + n) % 4), 2)]

    def y_first(a, h):
        for n in (2 * h, 2 * h + 1):
            start(chunk(MP.at[a, yf], n), chunk(R1.at[a], n), os_.at[a, n], or_.at[a, n], dev_y[n % 2])
        for n in (2 * h, 2 * h + 1):
            frm = (ym, yp)[n % 2]
            start(chunk(MP.at[a, frm], n), chunk(R2.at[a, 1 - n % 2], n),
                  os_.at[a, 4 + n], or_.at[a, 4 + n], dev_y[1 - n % 2])

    def y_second(a, h):
        for n in (2 * h, 2 * h + 1):
            to = (yp, ym)[n % 2]
            arrive(chunk(R1.at[a], n), or_.at[a, n])
            ks = pl.ds(2 * ((zh + n) % 4), 2)
            MP[a, to, ks] = (MP[a, to, ks].astype(F32) + R1[a, ks].astype(F32)).astype(BF16)
            start(chunk(MP.at[a, to], n), chunk(R2.at[a, n % 2], n), os2.at[a, n], or2.at[a, n], dev_y[n % 2])

    def y_last(a, h):
        for n in (2 * h, 2 * h + 1):
            to = (zh + n) % 4
            ks = pl.ds(2 * to, 2)
            arrive(chunk(R2.at[a, 1 - n % 2], n), or_.at[a, 4 + n])
            arrive(chunk(R2.at[a, n % 2], n), or2.at[a, n])
            total = MP[a, y, ks].astype(F32) + R2[a, 0, ks].astype(F32) + R2[a, 1, ks].astype(F32)
            ZS[a, ks] = total.astype(BF16)
            for cc in (0, 1):
                to_c = (c + cc) % 2
                cp = rc(ZS.at[a, 2 * to + to_c], ZR.at[a, z], es.at[a, 2 * n + cc], er.at[a, z],
                        did(x, y, 2 * to + c, to_c))
                if n or cc:
                    cp.start()
                    sent.append(cp)
                else:
                    @pl.when(home)
                    def _():
                        ZR[a, z] = ZS[a, 2 * zh + c]

                    @pl.when(away)
                    def _():
                        cp.start()
                    sent_away.append(cp)

    def finish_tokens(a, out):
        for dz in range(8):
            frm = (z + dz) % 8
            if dz:
                arrive(ZR.at[a, frm], er.at[a, frm])
            else:
                @pl.when(jnp.logical_not(home))
                def _():
                    arrive(ZR.at[a, frm], er.at[a, frm])
        total = ZR[a, 0].astype(F32)
        for s in range(1, 8):
            total = total + ZR[a, s].astype(F32)
        out[...] = total

    def wgrads(w, parity, store):
        def step(q, _):
            g = dot_nn(GTT[w], ROT[w // 2, 2 * q + parity].reshape(4 * ROWS, LANES))
            for p in range(4):
                store(p, q, g[p * UNITS:(p + 1) * UNITS])
            return 0
        lax.fori_loop(0, 4, step, 0)

    def wgrads_other(w):
        def store(p, q, g):
            CS[w, p, q] = g.astype(BF16)
        wgrads(w, other, store)
        start(CS.at[w], CR.at[w], cs.at[4 + w], cr.at[4 + w], here)

    def wgrads_own(w):
        def store(p, q, g):
            WO[w, p, q] = g
        wgrads(w, c, store)

    lo, hi = pl.ds(0, 2), pl.ds(2, 2)

    def x_first(w):
        arrive(CR.at[w], cr.at[4 + w])
        XS[w, xf] = (WO[w, xf] + CR[w, xf].astype(F32)).astype(BF16)
        start(XS.at[w, xf, lo], X1.at[w, 0], gs.at[w, 0], gr.at[w, 0], dev_x[0])
        start(XS.at[w, xf, hi], X1.at[w, 1], gs.at[w, 1], gr.at[w, 1], dev_x[1])
        XS[w, xp, 2:4] = (WO[w, xp, 2:4] + CR[w, xp, 2:4].astype(F32)).astype(BF16)
        start(XS.at[w, xp, hi], X2.at[w, 0, hi], gs.at[w, 2], gr.at[w, 2], dev_x[0])
        XS[w, xm, 0:2] = (WO[w, xm, 0:2] + CR[w, xm, 0:2].astype(F32)).astype(BF16)
        start(XS.at[w, xm, lo], X2.at[w, 1, lo], gs.at[w, 3], gr.at[w, 3], dev_x[1])

    def x_second(w):
        arrive(X1.at[w, 0], gr.at[w, 0])
        XS[w, xp, 0:2] = (WO[w, xp, 0:2] + CR[w, xp, 0:2].astype(F32) + X1[w, 0].astype(F32)).astype(BF16)
        start(XS.at[w, xp, lo], X2.at[w, 0, lo], gs.at[w, 4], gr.at[w, 4], dev_x[0])
        arrive(X1.at[w, 1], gr.at[w, 1])
        XS[w, xm, 2:4] = (WO[w, xm, 2:4] + CR[w, xm, 2:4].astype(F32) + X1[w, 1].astype(F32)).astype(BF16)
        start(XS.at[w, xm, hi], X2.at[w, 1, hi], gs.at[w, 5], gr.at[w, 5], dev_x[1])

    factor = 1.0 / math.sqrt(TOKENS)

    def x_last(w):
        arrive(X2.at[w, 0, hi], gr.at[w, 2])
        arrive(X2.at[w, 1, lo], gr.at[w, 3])
        arrive(X2.at[w, 0, lo], gr.at[w, 4])
        arrive(X2.at[w, 1, hi], gr.at[w, 5])
        total = WO[w, x] + CR[w, x].astype(F32) + X2[w, 0].astype(F32) + X2[w, 1].astype(F32)
        ZW[w] = (total * factor).astype(BF16)
        for q in (1, 3, 2):
            to = (zh + q) % 4
            start(ZW.at[w, to], ZWR.at[w, zh], vs.at[w, q], vr.at[w, q], did(x, y, 2 * to + zl, c))
        ZWR[w, zh] = ZW[w, zh]

    def finish_grad(w, out):
        for q in (1, 3, 2):
            arrive(ZWR.at[w, (zh + 4 - q) % 4], vr.at[w, q])
        rows = ZWR[w].reshape(4 * UNITS, LANES)
        out[...] = rows if w == 2 else rows.astype(F32).T.astype(BF16)

    def partial(a, h, left, matrix):
        for n in (2 * h, 2 * h + 1):
            for e in range(2):
                k = 2 * ((zh + n) % 4) + e
                MP[a, :, k] = dot_nn(left, matrix(k)).astype(BF16).reshape(4, ROWS, LANES)
        y_first(a, h)

    rotate_weight(2)
    partial(0, 0, hidden, lambda k: WR[2, k])
    partial(0, 1, hidden, lambda k: WR[2, k])
    rotate_in(1, y)
    rotate_in(1, ym)
    rotate_in(1, yp)
    rotate_weight(0)
    y_second(0, 0)
    rotate_weight(1)
    y_second(0, 1)
    tokens_far(1)
    wgrads_other(2)

    rot_grad = jnp.concatenate([rot(1, k) for k in range(8)], axis=1)
    grad_hidden = dot_nt(rot_grad, all_weight(2))
    gga = grad_hidden * GACT[0]
    gua = grad_hidden * GACT[1]
    both = jnp.concatenate([gga.astype(BF16), gua.astype(BF16)], axis=1)

    def gate_up(k):
        return jnp.concatenate([WR[0, k], WR[1, k]], axis=0)

    partial(1, 0, both, gate_up)
    partial(1, 1, both, gate_up)
    wgrads_own(2)
    GTT[0] = gga.T.astype(BF16)
    wgrads_other(0)
    x_first(2)
    GTT[1] = gua.T.astype(BF16)
    wgrads_other(1)
    wgrads_own(0)
    x_first(0)
    x_second(2)
    y_last(0, 0)
    y_second(1, 0)
    wgrads_own(1)
    x_first(1)
    y_last(0, 1)
    y_second(1, 1)
    x_second(0)
    x_last(2)
    y_last(1, 0)
    x_second(1)
    x_last(0)
    y_last(1, 1)
    x_last(1)
    finish_tokens(0, mixed)
    finish_grad(2, gd)
    finish_grad(0, gg)
    finish_tokens(1, gtok)
    finish_grad(1, gu)

    for cp in sent:
        cp.wait_send()

    @pl.when(home)
    def _():
        for cp in sent_home:
            cp.wait_send()

    @pl.when(away)
    def _():
        for cp in sent_away:
            cp.wait_send()


def copies(*refs):
    n = 5
    ins, outs, held, sems = refs[:n], refs[n:2 * n], refs[2 * n:3 * n], refs[3 * n]
    loads = [pltpu.make_async_copy(ins[i], held[i], sems.at[0, i]) for i in range(n)]
    stores = [pltpu.make_async_copy(held[i], outs[i], sems.at[1, i]) for i in range(n)]
    for cp in loads:
        cp.start()
    for i in range(n):
        loads[i].wait()
        stores[i].start()
    for cp in stores:
        cp.wait()


def shards(tokens, gate_weight, up_weight, down_weight, out_grad):
    dma = pltpu.SemaphoreType.DMA
    vm = pltpu.VMEM
    block = jax.ShapeDtypeStruct
    rows, cols = tokens.shape
    outs = (
        block((ROWS, LANES), F32), block((ROWS, LANES), F32),
        block((256, 256), BF16), block((256, 256), BF16), block((256, 256), BF16))
    results = pl.pallas_call(
        kernel,
        out_shape=outs,
        in_specs=[pl.BlockSpec(memory_space=pl.ANY)] * 5,
        out_specs=[pl.BlockSpec(memory_space=vm)] * 5,
        scratch_shapes=[
            vm((3, 256, 256), BF16),
            vm((2, ROWS, LANES), BF16),
            vm((2, 4, 8, ROWS, LANES), BF16),
            vm((4, 192, LANES), BF16),
            vm((4, 2, 4, 192, LANES), BF16),
            vm((LANES, LANES), BF16),
            vm((8, 256, LANES), F32),
            vm((3, 8, 256, LANES), BF16),
            vm((2, 8, 4, ROWS, LANES), BF16),
            vm((2, 4 * ROWS, 256), F32),
            vm((2, 4, 8, ROWS, LANES), BF16),
            vm((2, 8, ROWS, LANES), BF16),
            vm((2, 2, 8, ROWS, LANES), BF16),
            vm((2, 8, ROWS, LANES), BF16),
            vm((2, 8, ROWS, LANES), BF16),
            vm((3, 4, 4, UNITS, LANES), F32),
            vm((3, 4, 4, UNITS, LANES), BF16),
            vm((3, 4, 4, UNITS, LANES), BF16),
            vm((3, 4, 4, UNITS, LANES), BF16),
            vm((3, 2, 2, UNITS, LANES), BF16),
            vm((3, 2, 4, UNITS, LANES), BF16),
            vm((3, 4, UNITS, LANES), BF16),
            vm((3, 4, UNITS, LANES), BF16),
            vm((3, 256, 4 * ROWS), BF16),
            dma((5,)), dma((2, 3)), dma((2, 8)), dma((2, 2)), dma((2, 4)), dma((2, 2)), dma((2, 2)),
            dma((4,)), dma((4,)),
            dma((2, 4, 2)), dma((2, 4, 2)), dma((2, 4)), dma((2, 4)),
            dma((4, 3)), dma((4, 3)),
            dma((8,)), dma((8,)), dma((2, 8)), dma((2, 8)), dma((2, 4)), dma((2, 4)),
            dma((2, 8)), dma((2, 8)), dma((3, 6)), dma((3, 6)), dma((3, 4)), dma((3, 4)),
        ],
        compiler_params=pltpu.CompilerParams(
            collective_id=0, has_side_effects=True, vmem_limit_bytes=56 << 20),
        name="layer",
    )(tokens, out_grad, gate_weight, up_weight, down_weight)
    return pl.pallas_call(
        copies,
        out_shape=outs,
        in_specs=[pl.BlockSpec(memory_space=pltpu.HBM)] * 5,
        out_specs=[pl.BlockSpec(memory_space=pltpu.HBM)] * 5,
        scratch_shapes=[vm(o.shape, o.dtype) for o in outs] + [dma((2, 5))],
        compiler_params=pltpu.CompilerParams(vmem_limit_bytes=60 << 20),
        name="results",
    )(*results)


def solution(mesh):
    return jax.shard_map(
        shards,
        mesh=mesh,
        in_specs=(P("dp", "tensor"), P("tensor", "dp"), P("tensor", "dp"), P("dp", "tensor"), P("dp", "tensor")),
        out_specs=(P("dp", "tensor"), P("dp", "tensor"), P("tensor", "dp"), P("tensor", "dp"), P("dp", "tensor")),
        check_vma=False,
    )
```

```python
import math

import jax
import jax.numpy as jnp
from jax import lax
from jax.experimental import pallas as pl
from jax.experimental.pallas import tpu as pltpu
from jax.sharding import PartitionSpec as P

D = 2048
TOKENS = 2560
ROWS = 80
LANES = 256
UNITS = 64
MESH = pl.DeviceIdType.MESH
F32 = jnp.float32
BF16 = jnp.bfloat16


def dot_nn(a, b):
    return lax.dot_general(a, b, (((1,), (0,)), ((), ())), preferred_element_type=F32)


def dot_nt(a, b):
    return lax.dot_general(a, b, (((1,), (1,)), ((), ())), preferred_element_type=F32)


def butterflies(parts):
    parts = list(parts)
    for bit in range(3):
        step = 1 << bit
        for low in range(8):
            if not low & step:
                a, b = parts[low], parts[low | step]
                parts[low], parts[low | step] = a + b, a - b
    return parts


def kernel(tok_hbm, og_hbm, gw, uw, dw, mixed, gtok, gg, gu, gd,
           WIN, TIN, AB, PK, WB, H, FS, WR, ROT, GACT, MP, R1, R2, ZS, ZR, Q3, Q4, ZQ,
           WO, CS, CR, XS, X1, X2, ZW, ZWR, GTT,
           loads, zs, zr, zfs, zfr, zes, zer, ws, wr, ys, yr, y2s, y2r, xs, xr, cs, cr, os_, or_, os2, or2,
           es, er, q3s, q3r, q4s, q4r, gs, gr, vs, vr):
    dp = lax.axis_index("dp")
    te = lax.axis_index("tensor")
    x, zl, y = dp // 8, (dp // 4) % 2, dp % 4
    zh, c = te // 2, te % 2
    z = 2 * zh + zl
    k_own = te
    other = 1 - c
    home = c == zl
    xp, xm, xf = (x + 1) % 4, (x + 3) % 4, (x + 2) % 4
    yp, ym, yf = (y + 1) % 4, (y + 3) % 4, (y + 2) % 4

    def did(x_, y_, z_, c_):
        return ((x_ * 2 + z_ % 2) * 4 + y_, (z_ // 2) * 2 + c_)

    def rc(src, dst, send, recv, dev):
        return pltpu.make_async_remote_copy(
            src_ref=src, dst_ref=dst, send_sem=send, recv_sem=recv,
            device_id=dev, device_id_type=MESH)

    here = did(x, y, z, other)
    dev_x = (did(xp, y, z, c), did(xm, y, z, c), did(xf, y, z, c))
    dev_y = (did(x, yp, z, c), did(x, ym, z, c))
    sent, sent_home, sent_away = [], [], []

    def start(src, dst, send, recv, dev):
        cp = rc(src, dst, send, recv, dev)
        cp.start()
        sent.append(cp)

    def arrive(dst, recv):
        rc(dst, dst, recv, recv, here).wait_recv()

    barrier = pltpu.get_barrier_semaphore()

    def greet(dev):
        pl.semaphore_signal(barrier, inc=1, device_id=dev, device_id_type=MESH)

    for dz in range(8):
        for cc in range(2):
            if dz or cc:
                greet(did(x, y, (z + dz) % 8, (c + cc) % 2))
    for dev in dev_x + dev_y:
        greet(dev)

    fetched = [pltpu.make_async_copy(ref, WIN.at[n], loads.at[n]) for n, ref in enumerate((gw, uw, dw))]
    fetched_tokens = [pltpu.make_async_copy(ref, TIN.at[n], loads.at[3 + n]) for n, ref in enumerate((tok_hbm, og_hbm))]
    for cp in fetched_tokens + fetched:
        cp.start()
    tok, og = TIN.at[0], TIN.at[1]

    for cp in fetched_tokens:
        cp.wait()
    pl.semaphore_wait(barrier, 20)

    def signs():
        i = lax.broadcasted_iota(jnp.int32, (LANES, LANES), 0)
        j = lax.broadcasted_iota(jnp.int32, (LANES, LANES), 1)
        b = i & j
        b = b ^ (b >> 4)
        b = b ^ (b >> 2)
        b = (b ^ (b >> 1)) & 1
        H[...] = (1 - 2 * b).astype(F32).astype(BF16)

    def pack():
        for cp in fetched:
            cp.wait()
        gwt = WIN[0].astype(F32).T.astype(BF16)
        uwt = WIN[1].astype(F32).T.astype(BF16)
        for q in range(4):
            PK[q, 0:UNITS] = gwt[q * UNITS:(q + 1) * UNITS]
            PK[q, UNITS:2 * UNITS] = uwt[q * UNITS:(q + 1) * UNITS]
            PK[q, 2 * UNITS:3 * UNITS] = WIN[2, q * UNITS:(q + 1) * UNITS, :]
        WB[x, c, zh] = PK[zh]

    dev_z = (did(x, y, (z + 1) % 8, c), did(x, y, (z + 7) % 8, c))
    own_z = (did(x, y, (z + 1) % 8, zl), did(x, y, (z + 7) % 8, zl))
    away = jnp.logical_not(home)

    def send_tokens(a, ref):
        for way in range(2):
            start(ref, AB.at[a, y, k_own], zs.at[a, way], zr.at[a, k_own], own_z[way])

        cp = rc(ref, AB.at[a, y, k_own], zs.at[a, 2], zr.at[a, k_own], here)

        @pl.when(home)
        def _():
            pltpu.make_async_copy(ref, AB.at[a, y, k_own], zs.at[a, 2]).start()

        @pl.when(away)
        def _():
            cp.start()
        sent_away.append(cp)

    def send_weights(q):
        to = (zh + q) % 4
        start(PK.at[to], WB.at[x, c, zh], ws.at[q], wr.at[q], did(x, y, 2 * to + zl, c))

    shift = zl
    at_home = [zh, (zh + 3) % 4, (zh + 1) % 4, (zh + 2) % 4]
    at_away = [(zh + 3 + shift) % 4, (zh + shift) % 4, (zh + 2 + shift) % 4, (zh + 1 + shift) % 4]
    step_zh = [jnp.where(home, p, q) for p, q in zip(at_home, at_away)]

    def pair(a, yy, pos):
        return AB.at[a, yy, pl.ds(2 * step_zh[pos], 2)]

    def tokens_z(a, pos):
        near = step_zh[pos]
        one = [AB.at[a, y, 2 * near + n] for n in range(2)]
        both = pair(a, y, pos)
        sem = [zr.at[a, 2 * near + n] for n in range(2)]

        def relay(way):
            return rc(both, both, zfs.at[a, way], zfr.at[a, near], dev_z[way])

        def last(way):
            return rc(one[way], one[way], zes.at[a, way], zer.at[a, way], dev_z[way])

        if 0 < pos < 3:
            from_home = relay(pos - 1)
            sent_home.append(from_home)
        from_away = relay(pos) if pos < 2 else last(pos - 2)
        sent_away.append(from_away)

        @pl.when(home)
        def _():
            if pos == 0:
                arrive(AB.at[a, y, 2 * near + other], zr.at[a, 2 * near + other])
                pltpu.make_async_copy((tok, og)[a], AB.at[a, y, k_own], zs.at[a, 2]).wait()
            elif pos < 3:
                arrive(both, zfr.at[a, near])
                from_home.start()
            else:
                arrive(one[0], zer.at[a, 0])
                arrive(one[1], zer.at[a, 1])

        @pl.when(away)
        def _():
            if pos < 2:
                arrive(one[0], sem[0])
                arrive(one[1], sem[1])
                from_away.start()
            else:
                arrive(both, zfr.at[a, near])
                from_away.start()

    def tokens_out(a, pos):
        for way in range(2):
            start(pair(a, y, pos), pair(a, y, pos), ys.at[a, pos, way], yr.at[a, pos, way], dev_y[way])

    def weights_z(q):
        frm = (zh + 4 - q) % 4
        if q:
            arrive(WB.at[x, c, frm], wr.at[q])
        for way in range(3):
            start(WB.at[x, c, frm], WB.at[x, c, frm], xs.at[q, way], xr.at[q, way], dev_x[way])

    def to_core(n):
        frm = (x, xm, xp, xf)[n]
        if n:
            for q in range(4):
                arrive(WB.at[frm, c, (zh + 4 - q) % 4], xr.at[q, n - 1])
        start(WB.at[frm, c], WB.at[frm, c], cs.at[n], cr.at[n], here)

    def tokens_y(a, steps=range(4)):
        for pos in steps:
            for way in range(2):
                frm = (ym, yp)[way]
                arrive(pair(a, frm, pos), yr.at[a, pos, way])
                if (pos < 2) == (way == 0):
                    start(pair(a, frm, pos), pair(a, frm, pos), y2s.at[a, pos], y2r.at[a, pos], dev_y[way])

    def weights_far():
        for n, frm in enumerate((x, xm, xp, xf)):
            arrive(WB.at[frm, other], cr.at[n])

    scale = 1.0 / math.sqrt(D)

    def spread(a, yy):
        def step(r, _):
            rows = pl.ds(pl.multiple_of(r * 16, 16), 16)
            parts = butterflies([FS[k, rows] for k in range(8)])
            for k in range(8):
                ROT[a, k, yy, rows] = (parts[k] * scale).astype(BF16)
            return 0
        lax.fori_loop(0, ROWS // 16, step, 0)

    def rotate_in(a, yy):
        FS[:, 0:ROWS] = dot_nn(AB[a, yy].reshape(8 * ROWS, LANES), H[...]).reshape(8, ROWS, LANES)
        spread(a, yy)

    def tokens_far(a):
        for pos in range(4):
            arrive(pair(a, yf, pos), y2r.at[a, pos])
        rotate_in(a, yf)


    def rot(a, k):
        return ROT[a, k].reshape(4 * ROWS, LANES)

    def weight(w, k):
        return jnp.concatenate(
            [WB[q, k % 2, k // 2, w * UNITS:(w + 1) * UNITS] for q in range(4)], axis=0)

    def rotate_weight(w):
        for k in range(8):
            FS[k] = dot_nn(weight(w, k), H[...])

        def step(r, _):
            rows = pl.ds(pl.multiple_of(r * 16, 16), 16)
            parts = butterflies([FS[k, rows] for k in range(8)])
            for k in range(8):
                WR[w, k, rows] = (parts[k] * scale).astype(BF16)
            return 0
        lax.fori_loop(0, 256 // 16, step, 0)

    def all_weight(w):
        return jnp.concatenate([weight(w, k) for k in range(8)], axis=1)

    def all_rot(a):
        return jnp.concatenate([rot(a, k) for k in range(8)], axis=1)

    kept = {}

    def gates():
        tokens = all_rot(0)
        gate = dot_nt(tokens, all_weight(0))
        up = dot_nt(tokens, all_weight(1))
        sigma = 1.0 / (1.0 + jnp.exp(-gate))
        hidden = gate * sigma * up
        kept[0] = hidden.astype(BF16)
        GTT[2] = hidden.T.astype(BF16)
        GACT[0] = up * sigma * (1.0 + gate * (1.0 - sigma))
        GACT[1] = gate * sigma

    def hidden_grads():
        grad_hidden = dot_nt(all_rot(1), all_weight(2))
        kept["gate"] = grad_hidden * GACT[0]
        kept["up"] = grad_hidden * GACT[1]
        kept[1] = jnp.concatenate([kept["gate"].astype(BF16), kept["up"].astype(BF16)], axis=1)

    def turn(w):
        GTT[w] = kept[("gate", "up")[w]].T.astype(BF16)

    def partial(a, h):
        for n in (2 * h, 2 * h + 1):
            for e in range(2):
                k = 2 * ((zh + n) % 4) + e
                matrix = jnp.concatenate([WR[0, k], WR[1, k]], axis=0) if a else WR[2, k]
                MP[a, :, k] = dot_nn(kept[a], matrix).astype(BF16).reshape(4, ROWS, LANES)
        y_first(a, h)

    def chunk(ref, n):
        return ref.at[pl.ds(2 * ((zh + n) % 4), 2)]

    def y_first(a, h):
        for n in (2 * h, 2 * h + 1):
            start(chunk(MP.at[a, yf], n), chunk(R1.at[a], n), os_.at[a, n], or_.at[a, n], dev_y[n % 2])
        for n in (2 * h, 2 * h + 1):
            frm = (ym, yp)[n % 2]
            start(chunk(MP.at[a, frm], n), chunk(R2.at[a, 1 - n % 2], n),
                  os_.at[a, 4 + n], or_.at[a, 4 + n], dev_y[1 - n % 2])

    def y_second(a, h):
        for n in (2 * h, 2 * h + 1):
            to = (yp, ym)[n % 2]
            arrive(chunk(R1.at[a], n), or_.at[a, n])
            ks = pl.ds(2 * ((zh + n) % 4), 2)
            MP[a, to, ks] = (MP[a, to, ks].astype(F32) + R1[a, ks].astype(F32)).astype(BF16)
            start(chunk(MP.at[a, to], n), chunk(R2.at[a, n % 2], n), os2.at[a, n], or2.at[a, n], dev_y[n % 2])

    def near_z(n):
        return did(x, y, (z + n) % 8, c)

    def owner(n, cc):
        return did(x, y, (z + n) % 8, cc)

    def to_zh(n):
        return (zh + n) % 4

    def y_last(a):
        for n in range(4):
            ks = pl.ds(2 * to_zh(n), 2)
            arrive(chunk(R2.at[a, 1 - n % 2], n), or_.at[a, 4 + n])
            arrive(chunk(R2.at[a, n % 2], n), or2.at[a, n])
            total = MP[a, y, ks].astype(F32) + R2[a, 0, ks].astype(F32) + R2[a, 1, ks].astype(F32)
            ZS[a, ks] = total.astype(BF16)
        far = [rc(ZS.at[a, 2 * to_zh(2) + w], Q4.at[a, w], q4s.at[a, w], q4r.at[a, w], near_z((2, 6)[w]))
               for w in range(2)]
        own = rc(ZS.at[a, 2 * zh + other], ZR.at[a, 0], es.at[a, 0], er.at[a, 0], here)
        thirds = [rc(ZS.at[a, pl.ds(2 * to_zh((1, 2)[w] + zl), 2)], Q3.at[a, w], q3s.at[a, w], q3r.at[a, w],
                     near_z((1, 7)[w])) for w in range(2)]
        firsts = [rc(ZS.at[a, 2 * to_zh((0, 3)[w] + zl) + cc], ZR.at[a, 1 + w], es.at[a, 1 + 2 * w + cc],
                     er.at[a, 1 + w], owner((1, 7)[w], cc)) for w in range(2) for cc in range(2)]
        sent_home.extend(far + [own])
        sent_away.extend(thirds + firsts)

        @pl.when(home)
        def _():
            for cp in far:
                cp.start()
            own.start()
            ZR[a, 0] = ZS[a, 2 * zh + c]

        @pl.when(away)
        def _():
            for cp in thirds + firsts:
                cp.start()

    def z_second(a):
        seconds = [rc(ZQ.at[a, w, cc], ZR.at[a, 3 + w], es.at[a, 5 + 2 * w + cc], er.at[a, 3 + w],
                      owner((2, 6)[w], cc)) for w in range(2) for cc in range(2)]
        sent_home.extend(seconds)

        @pl.when(home)
        def _():
            for w in range(2):
                arrive(Q3.at[a, w], q3r.at[a, w])
                arrive(Q4.at[a, w], q4r.at[a, w])
                for cc in range(2):
                    total = ZS[a, 2 * to_zh((1, 3)[w]) + cc].astype(F32) + Q3[a, w, cc].astype(F32)
                    if cc == w:
                        total = total + Q4[a, w].astype(F32)
                    ZQ[a, w, cc] = total.astype(BF16)
                    seconds[2 * w + cc].start()

    def finish_tokens(a, out):
        @pl.when(away)
        def _():
            arrive(ZR.at[a, 0], er.at[a, 0])
        total = ZR[a, 0].astype(F32)
        for n in range(1, 5):
            arrive(ZR.at[a, n], er.at[a, n])
            total = total + ZR[a, n].astype(F32)
        out[...] = total

    def wgrads(w, parity, store):
        def step(q, _):
            g = dot_nn(GTT[w], ROT[w // 2, 2 * q + parity].reshape(4 * ROWS, LANES))
            for p in range(4):
                store(p, q, g[p * UNITS:(p + 1) * UNITS])
            return 0
        lax.fori_loop(0, 4, step, 0)

    def wgrads_other(w):
        def store(p, q, g):
            CS[w, p, q] = g.astype(BF16)
        wgrads(w, other, store)
        start(CS.at[w], CR.at[w], cs.at[4 + w], cr.at[4 + w], here)

    def wgrads_own(w):
        def store(p, q, g):
            WO[w, p, q] = g
        wgrads(w, c, store)

    lo, hi = pl.ds(0, 2), pl.ds(2, 2)

    def x_first(w):
        arrive(CR.at[w], cr.at[4 + w])
        XS[w, xf] = (WO[w, xf] + CR[w, xf].astype(F32)).astype(BF16)
        start(XS.at[w, xf, lo], X1.at[w, 0], gs.at[w, 0], gr.at[w, 0], dev_x[0])
        start(XS.at[w, xf, hi], X1.at[w, 1], gs.at[w, 1], gr.at[w, 1], dev_x[1])
        XS[w, xp, 2:4] = (WO[w, xp, 2:4] + CR[w, xp, 2:4].astype(F32)).astype(BF16)
        start(XS.at[w, xp, hi], X2.at[w, 0, hi], gs.at[w, 2], gr.at[w, 2], dev_x[0])
        XS[w, xm, 0:2] = (WO[w, xm, 0:2] + CR[w, xm, 0:2].astype(F32)).astype(BF16)
        start(XS.at[w, xm, lo], X2.at[w, 1, lo], gs.at[w, 3], gr.at[w, 3], dev_x[1])

    def x_second(w):
        arrive(X1.at[w, 0], gr.at[w, 0])
        XS[w, xp, 0:2] = (WO[w, xp, 0:2] + CR[w, xp, 0:2].astype(F32) + X1[w, 0].astype(F32)).astype(BF16)
        start(XS.at[w, xp, lo], X2.at[w, 0, lo], gs.at[w, 4], gr.at[w, 4], dev_x[0])
        arrive(X1.at[w, 1], gr.at[w, 1])
        XS[w, xm, 2:4] = (WO[w, xm, 2:4] + CR[w, xm, 2:4].astype(F32) + X1[w, 1].astype(F32)).astype(BF16)
        start(XS.at[w, xm, hi], X2.at[w, 1, hi], gs.at[w, 5], gr.at[w, 5], dev_x[1])

    factor = 1.0 / math.sqrt(TOKENS)

    def x_last(w):
        arrive(X2.at[w, 0, hi], gr.at[w, 2])
        arrive(X2.at[w, 1, lo], gr.at[w, 3])
        arrive(X2.at[w, 0, lo], gr.at[w, 4])
        arrive(X2.at[w, 1, hi], gr.at[w, 5])
        total = WO[w, x] + CR[w, x].astype(F32) + X2[w, 0].astype(F32) + X2[w, 1].astype(F32)
        ZW[w] = (total * factor).astype(BF16)
        for q in (1, 3, 2):
            to = (zh + q) % 4
            start(ZW.at[w, to], ZWR.at[w, zh], vs.at[w, q], vr.at[w, q], did(x, y, 2 * to + zl, c))
        ZWR[w, zh] = ZW[w, zh]

    def finish_grad(w, out):
        for q in (1, 3, 2):
            arrive(ZWR.at[w, (zh + 4 - q) % 4], vr.at[w, q])
        rows = ZWR[w].reshape(4 * UNITS, LANES)
        out[...] = rows if w == 2 else rows.astype(F32).T.astype(BF16)

    send_tokens(0, tok)
    send_tokens(1, og)
    pack()
    send_weights(1)
    send_weights(3)
    weights_z(0)
    signs()
    tokens_z(0, 0)
    tokens_out(0, 0)
    tokens_z(1, 0)
    tokens_out(1, 0)
    tokens_z(0, 1)
    tokens_out(0, 1)
    tokens_z(1, 1)
    tokens_out(1, 1)
    send_weights(2)
    weights_z(1)
    weights_z(3)
    tokens_z(0, 2)
    tokens_out(0, 2)
    tokens_z(1, 2)
    tokens_out(1, 2)
    tokens_z(0, 3)
    tokens_out(0, 3)
    tokens_z(1, 3)
    tokens_out(1, 3)
    weights_z(2)
    tokens_y(0, (0,))
    tokens_y(0, (1,))
    tokens_y(0, (2,))
    tokens_y(0, (3,))
    rotate_in(0, y)
    rotate_in(0, ym)
    tokens_y(1, (0,))
    tokens_y(1, (1,))
    tokens_y(1, (2,))
    tokens_y(1, (3,))
    rotate_in(0, yp)
    to_core(0)
    to_core(1)
    to_core(2)
    to_core(3)
    tokens_far(0)
    weights_far()
    gates()
    rotate_weight(2)
    partial(0, 0)
    partial(0, 1)
    rotate_in(1, y)
    rotate_in(1, ym)
    rotate_in(1, yp)
    rotate_weight(0)
    rotate_weight(1)
    tokens_far(1)
    wgrads_other(2)
    hidden_grads()
    y_second(0, 0)
    y_second(0, 1)
    partial(1, 0)
    partial(1, 1)
    wgrads_own(2)
    x_first(2)
    turn(0)
    wgrads_other(0)
    wgrads_own(0)
    x_second(2)
    y_last(0)
    turn(1)
    wgrads_other(1)
    x_first(0)
    wgrads_own(1)
    x_last(2)
    z_second(0)
    y_second(1, 0)
    y_second(1, 1)
    x_first(1)
    x_second(0)
    x_last(0)
    x_second(1)
    y_last(1)
    x_last(1)
    finish_tokens(0, mixed)
    finish_grad(2, gd)
    z_second(1)
    finish_grad(0, gg)
    finish_grad(1, gu)
    finish_tokens(1, gtok)

    for cp in sent:
        cp.wait_send()

    @pl.when(home)
    def _():
        for cp in sent_home:
            cp.wait_send()

    @pl.when(away)
    def _():
        for cp in sent_away:
            cp.wait_send()


def copies(*refs):
    n = 5
    ins, outs, held, sems = refs[:n], refs[n:2 * n], refs[2 * n:3 * n], refs[3 * n]
    loads = [pltpu.make_async_copy(ins[i], held[i], sems.at[0, i]) for i in range(n)]
    stores = [pltpu.make_async_copy(held[i], outs[i], sems.at[1, i]) for i in range(n)]
    for cp in loads:
        cp.start()
    for i in range(n):
        loads[i].wait()
        stores[i].start()
    for cp in stores:
        cp.wait()


def shards(tokens, gate_weight, up_weight, down_weight, out_grad):
    dma = pltpu.SemaphoreType.DMA
    vm = pltpu.VMEM
    block = jax.ShapeDtypeStruct
    rows, cols = tokens.shape
    outs = (
        block((ROWS, LANES), F32), block((ROWS, LANES), F32),
        block((256, 256), BF16), block((256, 256), BF16), block((256, 256), BF16))
    results = pl.pallas_call(
        kernel,
        out_shape=outs,
        in_specs=[pl.BlockSpec(memory_space=pl.ANY)] * 5,
        out_specs=[pl.BlockSpec(memory_space=vm)] * 5,
        scratch_shapes=[
            vm((3, 256, 256), BF16),
            vm((2, ROWS, LANES), BF16),
            vm((2, 4, 8, ROWS, LANES), BF16),
            vm((4, 192, LANES), BF16),
            vm((4, 2, 4, 192, LANES), BF16),
            vm((LANES, LANES), BF16),
            vm((8, 256, LANES), F32),
            vm((3, 8, 256, LANES), BF16),
            vm((2, 8, 4, ROWS, LANES), BF16),
            vm((2, 4 * ROWS, 256), F32),
            vm((2, 4, 8, ROWS, LANES), BF16),
            vm((2, 8, ROWS, LANES), BF16),
            vm((2, 2, 8, ROWS, LANES), BF16),
            vm((2, 8, ROWS, LANES), BF16),
            vm((2, 5, ROWS, LANES), BF16),
            vm((2, 2, 2, ROWS, LANES), BF16),
            vm((2, 2, ROWS, LANES), BF16),
            vm((2, 2, 2, ROWS, LANES), BF16),
            vm((3, 4, 4, UNITS, LANES), F32),
            vm((3, 4, 4, UNITS, LANES), BF16),
            vm((3, 4, 4, UNITS, LANES), BF16),
            vm((3, 4, 4, UNITS, LANES), BF16),
            vm((3, 2, 2, UNITS, LANES), BF16),
            vm((3, 2, 4, UNITS, LANES), BF16),
            vm((3, 4, UNITS, LANES), BF16),
            vm((3, 4, UNITS, LANES), BF16),
            vm((3, 256, 4 * ROWS), BF16),
            dma((5,)), dma((2, 3)), dma((2, 8)), dma((2, 2)), dma((2, 4)), dma((2, 2)), dma((2, 2)),
            dma((4,)), dma((4,)),
            dma((2, 4, 2)), dma((2, 4, 2)), dma((2, 4)), dma((2, 4)),
            dma((4, 3)), dma((4, 3)),
            dma((8,)), dma((8,)), dma((2, 8)), dma((2, 8)), dma((2, 4)), dma((2, 4)),
            dma((2, 9)), dma((2, 5)), dma((2, 2)), dma((2, 2)), dma((2, 2)), dma((2, 2)), dma((3, 6)), dma((3, 6)), dma((3, 4)), dma((3, 4)),
        ],
        compiler_params=pltpu.CompilerParams(
            collective_id=0, has_side_effects=True, vmem_limit_bytes=56 << 20),
        name="layer",
    )(tokens, out_grad, gate_weight, up_weight, down_weight)
    return pl.pallas_call(
        copies,
        out_shape=outs,
        in_specs=[pl.BlockSpec(memory_space=pltpu.HBM)] * 5,
        out_specs=[pl.BlockSpec(memory_space=pltpu.HBM)] * 5,
        scratch_shapes=[vm(o.shape, o.dtype) for o in outs] + [dma((2, 5))],
        compiler_params=pltpu.CompilerParams(vmem_limit_bytes=60 << 20),
        name="results",
    )(*results)


def solution(mesh):
    return jax.shard_map(
        shards,
        mesh=mesh,
        in_specs=(P("dp", "tensor"), P("tensor", "dp"), P("tensor", "dp"), P("dp", "tensor"), P("dp", "tensor")),
        out_specs=(P("dp", "tensor"), P("dp", "tensor"), P("tensor", "dp"), P("tensor", "dp"), P("dp", "tensor")),
        check_vma=False,
    )
```

```python
import math

import jax
import jax.numpy as jnp
from jax import lax
from jax.experimental import pallas as pl
from jax.experimental.pallas import tpu as pltpu
from jax.sharding import PartitionSpec as P

D = 2048
TOKENS = 2560
ROWS = 80
LANES = 256
UNITS = 64
MESH = pl.DeviceIdType.MESH
F32 = jnp.float32
BF16 = jnp.bfloat16


def dot_nn(a, b):
    return lax.dot_general(a, b, (((1,), (0,)), ((), ())), preferred_element_type=F32)


def dot_nt(a, b):
    return lax.dot_general(a, b, (((1,), (1,)), ((), ())), preferred_element_type=F32)


def butterflies(parts):
    parts = list(parts)
    for bit in range(3):
        step = 1 << bit
        for low in range(8):
            if not low & step:
                a, b = parts[low], parts[low | step]
                parts[low], parts[low | step] = a + b, a - b
    return parts


def kernel(tok_hbm, og_hbm, gw, uw, dw, mixed, gtok, gg, gu, gd,
           WIN, TIN, AB, PK, WB, H, FS, WR, ROT, GACT, MP, R1, R2, ZS, ZR, Q3, Q4, ZQ,
           WO, CS, CR, XS, X2, ZW, ZWR, GTT,
           loads, zs, zr, zfs, zfr, zes, zer, ws, wr, ys, yr, y2s, y2r, xs, xr, cs, cr, os_, or_, os2, or2,
           TOUT, GOUT, outs, es, er, q3s, q3r, q4s, q4r, gs, gr, vs, vr):
    dp = lax.axis_index("dp")
    te = lax.axis_index("tensor")
    x, zl, y = dp // 8, (dp // 4) % 2, dp % 4
    zh, c = te // 2, te % 2
    z = 2 * zh + zl
    k_own = te
    other = 1 - c
    home = c == zl
    xp, xm, xf = (x + 1) % 4, (x + 3) % 4, (x + 2) % 4
    yp, ym, yf = (y + 1) % 4, (y + 3) % 4, (y + 2) % 4

    def did(x_, y_, z_, c_):
        return ((x_ * 2 + z_ % 2) * 4 + y_, (z_ // 2) * 2 + c_)

    def rc(src, dst, send, recv, dev):
        return pltpu.make_async_remote_copy(
            src_ref=src, dst_ref=dst, send_sem=send, recv_sem=recv,
            device_id=dev, device_id_type=MESH)

    here = did(x, y, z, other)
    dev_x = (did(xp, y, z, c), did(xm, y, z, c), did(xf, y, z, c))
    dev_y = (did(x, yp, z, c), did(x, ym, z, c))
    sent, sent_home, sent_away = [], [], []

    def start(src, dst, send, recv, dev):
        cp = rc(src, dst, send, recv, dev)
        cp.start()
        sent.append(cp)

    leaving = []

    def leave(src, dst, n):
        cp = pltpu.make_async_copy(src, dst, outs.at[n])
        cp.start()
        leaving.append(cp)

    def arrive(dst, recv):
        rc(dst, dst, recv, recv, here).wait_recv()

    barrier = pltpu.get_barrier_semaphore()

    def greet(dev):
        pl.semaphore_signal(barrier, inc=1, device_id=dev, device_id_type=MESH)

    for dz in range(8):
        for cc in range(2):
            if dz or cc:
                greet(did(x, y, (z + dz) % 8, (c + cc) % 2))
    for dev in dev_x + dev_y:
        greet(dev)

    fetched = [pltpu.make_async_copy(ref, WIN.at[n], loads.at[n]) for n, ref in enumerate((gw, uw, dw))]
    fetched_tokens = [pltpu.make_async_copy(ref, TIN.at[n], loads.at[3 + n]) for n, ref in enumerate((tok_hbm, og_hbm))]
    for cp in fetched_tokens + fetched:
        cp.start()
    tok, og = TIN.at[0], TIN.at[1]

    for cp in fetched_tokens:
        cp.wait()
    pl.semaphore_wait(barrier, 20)

    def signs():
        i = lax.broadcasted_iota(jnp.int32, (LANES, LANES), 0)
        j = lax.broadcasted_iota(jnp.int32, (LANES, LANES), 1)
        b = i & j
        b = b ^ (b >> 4)
        b = b ^ (b >> 2)
        b = (b ^ (b >> 1)) & 1
        H[...] = (1 - 2 * b).astype(F32).astype(BF16)

    def pack():
        for cp in fetched:
            cp.wait()
        gwt = WIN[0].astype(F32).T.astype(BF16)
        uwt = WIN[1].astype(F32).T.astype(BF16)
        for q in range(4):
            PK[q, 0:UNITS] = gwt[q * UNITS:(q + 1) * UNITS]
            PK[q, UNITS:2 * UNITS] = uwt[q * UNITS:(q + 1) * UNITS]
            PK[q, 2 * UNITS:3 * UNITS] = WIN[2, q * UNITS:(q + 1) * UNITS, :]
        WB[x, c, zh] = PK[zh]

    dev_z = (did(x, y, (z + 1) % 8, c), did(x, y, (z + 7) % 8, c))
    own_z = (did(x, y, (z + 1) % 8, zl), did(x, y, (z + 7) % 8, zl))
    away = jnp.logical_not(home)

    def send_tokens(a, ref):
        for way in range(2):
            start(ref, AB.at[a, y, k_own], zs.at[a, way], zr.at[a, k_own], own_z[way])

        cp = rc(ref, AB.at[a, y, k_own], zs.at[a, 2], zr.at[a, k_own], here)

        @pl.when(home)
        def _():
            pltpu.make_async_copy(ref, AB.at[a, y, k_own], zs.at[a, 2]).start()

        @pl.when(away)
        def _():
            cp.start()
        sent_away.append(cp)

    def send_weights(q):
        to = (zh + q) % 4
        start(PK.at[to], WB.at[x, c, zh], ws.at[q], wr.at[q], did(x, y, 2 * to + zl, c))

    shift = zl
    at_home = [zh, (zh + 3) % 4, (zh + 1) % 4, (zh + 2) % 4]
    at_away = [(zh + 3 + shift) % 4, (zh + shift) % 4, (zh + 2 + shift) % 4, (zh + 1 + shift) % 4]
    step_zh = [jnp.where(home, p, q) for p, q in zip(at_home, at_away)]

    def pair(a, yy, pos):
        return AB.at[a, yy, pl.ds(2 * step_zh[pos], 2)]

    def tokens_z(a, pos):
        near = step_zh[pos]
        one = [AB.at[a, y, 2 * near + n] for n in range(2)]
        both = pair(a, y, pos)
        sem = [zr.at[a, 2 * near + n] for n in range(2)]

        def relay(way):
            return rc(both, both, zfs.at[a, way], zfr.at[a, near], dev_z[way])

        def last(way):
            return rc(one[way], one[way], zes.at[a, way], zer.at[a, way], dev_z[way])

        if 0 < pos < 3:
            from_home = relay(pos - 1)
            sent_home.append(from_home)
        from_away = relay(pos) if pos < 2 else last(pos - 2)
        sent_away.append(from_away)

        @pl.when(home)
        def _():
            if pos == 0:
                arrive(AB.at[a, y, 2 * near + other], zr.at[a, 2 * near + other])
                pltpu.make_async_copy((tok, og)[a], AB.at[a, y, k_own], zs.at[a, 2]).wait()
            elif pos < 3:
                arrive(both, zfr.at[a, near])
                from_home.start()
            else:
                arrive(one[0], zer.at[a, 0])
                arrive(one[1], zer.at[a, 1])

        @pl.when(away)
        def _():
            if pos < 2:
                arrive(one[0], sem[0])
                arrive(one[1], sem[1])
                from_away.start()
            else:
                arrive(both, zfr.at[a, near])
                from_away.start()

    def tokens_out(a, pos):
        for way in range(2):
            start(pair(a, y, pos), pair(a, y, pos), ys.at[a, pos, way], yr.at[a, pos, way], dev_y[way])

    def weights_z(q):
        frm = (zh + 4 - q) % 4
        if q:
            arrive(WB.at[x, c, frm], wr.at[q])
        for way in range(3):
            start(WB.at[x, c, frm], WB.at[x, c, frm], xs.at[q, way], xr.at[q, way], dev_x[way])

    def to_core(n):
        frm = (x, xm, xp, xf)[n]
        if n:
            for q in range(4):
                arrive(WB.at[frm, c, (zh + 4 - q) % 4], xr.at[q, n - 1])
        start(WB.at[frm, c], WB.at[frm, c], cs.at[n], cr.at[n], here)

    def tokens_y(a, steps=range(4)):
        for pos in steps:
            for way in range(2):
                frm = (ym, yp)[way]
                arrive(pair(a, frm, pos), yr.at[a, pos, way])
                if (pos < 2) == (way == 0):
                    start(pair(a, frm, pos), pair(a, frm, pos), y2s.at[a, pos], y2r.at[a, pos], dev_y[way])

    def weights_far():
        for n, frm in enumerate((x, xm, xp, xf)):
            arrive(WB.at[frm, other], cr.at[n])

    scale = 1.0 / math.sqrt(D)

    def spread(a, yy):
        def step(r, _):
            rows = pl.ds(pl.multiple_of(r * 16, 16), 16)
            parts = butterflies([FS[k, rows] for k in range(8)])
            for k in range(8):
                ROT[a, k, yy, rows] = (parts[k] * scale).astype(BF16)
            return 0
        lax.fori_loop(0, ROWS // 16, step, 0)

    def rotate_in(a, yy):
        FS[:, 0:ROWS] = dot_nn(AB[a, yy].reshape(8 * ROWS, LANES), H[...]).reshape(8, ROWS, LANES)
        spread(a, yy)

    def tokens_far(a):
        for pos in range(4):
            arrive(pair(a, yf, pos), y2r.at[a, pos])
        rotate_in(a, yf)


    def rot(a, k):
        return ROT[a, k].reshape(4 * ROWS, LANES)

    def weight(w, k):
        return jnp.concatenate(
            [WB[q, k % 2, k // 2, w * UNITS:(w + 1) * UNITS] for q in range(4)], axis=0)

    def rotate_weight(w):
        for k in range(8):
            FS[k] = dot_nn(weight(w, k), H[...])

        def step(r, _):
            rows = pl.ds(pl.multiple_of(r * 16, 16), 16)
            parts = butterflies([FS[k, rows] for k in range(8)])
            for k in range(8):
                WR[w, k, rows] = (parts[k] * scale).astype(BF16)
            return 0
        lax.fori_loop(0, 256 // 16, step, 0)

    def all_weight(w):
        return jnp.concatenate([weight(w, k) for k in range(8)], axis=1)

    def all_rot(a):
        return jnp.concatenate([rot(a, k) for k in range(8)], axis=1)

    kept = {}

    def gates():
        tokens = all_rot(0)
        gate = dot_nt(tokens, all_weight(0))
        up = dot_nt(tokens, all_weight(1))
        sigma = 1.0 / (1.0 + jnp.exp(-gate))
        hidden = gate * sigma * up
        kept[0] = hidden.astype(BF16)
        GTT[2] = hidden.T.astype(BF16)
        GACT[0] = up * sigma * (1.0 + gate * (1.0 - sigma))
        GACT[1] = gate * sigma

    def hidden_grads():
        grad_hidden = dot_nt(all_rot(1), all_weight(2))
        kept["gate"] = grad_hidden * GACT[0]
        kept["up"] = grad_hidden * GACT[1]
        kept[1] = jnp.concatenate([kept["gate"].astype(BF16), kept["up"].astype(BF16)], axis=1)

    def turn(w):
        GTT[w] = kept[("gate", "up")[w]].T.astype(BF16)

    def partial(a, h):
        for n in (2 * h, 2 * h + 1):
            for e in range(2):
                k = 2 * ((zh + n) % 4) + e
                matrix = jnp.concatenate([WR[0, k], WR[1, k]], axis=0) if a else WR[2, k]
                MP[a, :, k] = dot_nn(kept[a], matrix).astype(BF16).reshape(4, ROWS, LANES)
        y_first(a, h)

    def chunk(ref, n):
        return ref.at[pl.ds(2 * ((zh + n) % 4), 2)]

    def y_first(a, h):
        for n in (2 * h, 2 * h + 1):
            start(chunk(MP.at[a, yf], n), chunk(R1.at[a], n), os_.at[a, n], or_.at[a, n], dev_y[n % 2])
        for n in (2 * h, 2 * h + 1):
            frm = (ym, yp)[n % 2]
            start(chunk(MP.at[a, frm], n), chunk(R2.at[a, 1 - n % 2], n),
                  os_.at[a, 4 + n], or_.at[a, 4 + n], dev_y[1 - n % 2])

    def y_second(a, h):
        for n in (2 * h, 2 * h + 1):
            to = (yp, ym)[n % 2]
            arrive(chunk(R1.at[a], n), or_.at[a, n])
            ks = pl.ds(2 * ((zh + n) % 4), 2)
            MP[a, to, ks] = (MP[a, to, ks].astype(F32) + R1[a, ks].astype(F32)).astype(BF16)
            start(chunk(MP.at[a, to], n), chunk(R2.at[a, n % 2], n), os2.at[a, n], or2.at[a, n], dev_y[n % 2])

    def near_z(n):
        return did(x, y, (z + n) % 8, c)

    def owner(n, cc):
        return did(x, y, (z + n) % 8, cc)

    def to_zh(n):
        return (zh + n) % 4

    def y_last(a):
        for n in range(4):
            ks = pl.ds(2 * to_zh(n), 2)
            arrive(chunk(R2.at[a, 1 - n % 2], n), or_.at[a, 4 + n])
            arrive(chunk(R2.at[a, n % 2], n), or2.at[a, n])
            total = MP[a, y, ks].astype(F32) + R2[a, 0, ks].astype(F32) + R2[a, 1, ks].astype(F32)
            ZS[a, ks] = total.astype(BF16)
        far = [rc(ZS.at[a, 2 * to_zh(2) + w], Q4.at[a, w], q4s.at[a, w], q4r.at[a, w], near_z((2, 6)[w]))
               for w in range(2)]
        own = rc(ZS.at[a, 2 * zh + other], ZR.at[a, 0], es.at[a, 0], er.at[a, 0], here)
        thirds = [rc(ZS.at[a, pl.ds(2 * to_zh((1, 2)[w] + zl), 2)], Q3.at[a, w], q3s.at[a, w], q3r.at[a, w],
                     near_z((1, 7)[w])) for w in range(2)]
        firsts = [rc(ZS.at[a, 2 * to_zh((0, 3)[w] + zl) + cc], ZR.at[a, 1 + w], es.at[a, 1 + 2 * w + cc],
                     er.at[a, 1 + w], owner((1, 7)[w], cc)) for w in range(2) for cc in range(2)]
        sent_home.extend(far + [own])
        sent_away.extend(thirds + firsts)

        @pl.when(home)
        def _():
            for cp in far:
                cp.start()
            own.start()
            ZR[a, 0] = ZS[a, 2 * zh + c]

        @pl.when(away)
        def _():
            for cp in thirds + firsts:
                cp.start()

    def z_second(a):
        seconds = [rc(ZQ.at[a, w, cc], ZR.at[a, 3 + w], es.at[a, 5 + 2 * w + cc], er.at[a, 3 + w],
                      owner((2, 6)[w], cc)) for w in range(2) for cc in range(2)]
        sent_home.extend(seconds)

        @pl.when(home)
        def _():
            for w in range(2):
                arrive(Q3.at[a, w], q3r.at[a, w])
                arrive(Q4.at[a, w], q4r.at[a, w])
                for cc in range(2):
                    total = ZS[a, 2 * to_zh((1, 3)[w]) + cc].astype(F32) + Q3[a, w, cc].astype(F32)
                    if cc == w:
                        total = total + Q4[a, w].astype(F32)
                    ZQ[a, w, cc] = total.astype(BF16)
                    seconds[2 * w + cc].start()

    def finish_tokens(a, out):
        @pl.when(away)
        def _():
            arrive(ZR.at[a, 0], er.at[a, 0])
        total = ZR[a, 0].astype(F32)
        for n in range(1, 5):
            arrive(ZR.at[a, n], er.at[a, n])
            total = total + ZR[a, n].astype(F32)
        TOUT[a] = total
        leave(TOUT.at[a], out, a)

    def wgrads(w, parity, store):
        def step(q, _):
            g = dot_nn(GTT[w], ROT[w // 2, 2 * q + parity].reshape(4 * ROWS, LANES))
            for p in range(4):
                store(p, q, g[p * UNITS:(p + 1) * UNITS])
            return 0
        lax.fori_loop(0, 4, step, 0)

    def wgrads_other(w):
        def store(p, q, g):
            CS[w, p, q] = g.astype(BF16)
        wgrads(w, other, store)
        start(CS.at[w], CR.at[w], cs.at[4 + w], cr.at[4 + w], here)

    def wgrads_own(w):
        def store(p, q, g):
            WO[w, p, q] = g
        wgrads(w, c, store)

    def x_first(w):
        arrive(CR.at[w], cr.at[4 + w])
        for n, to in enumerate((xp, xm, xf)):
            XS[w, to] = (WO[w, to] + CR[w, to].astype(F32)).astype(BF16)
            start(XS.at[w, to], X2.at[w, n], gs.at[w, n], gr.at[w, n], dev_x[n])

    factor = 1.0 / math.sqrt(TOKENS)

    def x_last(w):
        total = WO[w, x] + CR[w, x].astype(F32)
        for n in range(3):
            arrive(X2.at[w, n], gr.at[w, n])
            total = total + X2[w, n].astype(F32)
        ZW[w] = (total * factor).astype(BF16)
        for q in (1, 3, 2):
            to = (zh + q) % 4
            start(ZW.at[w, to], ZWR.at[w, zh], vs.at[w, q], vr.at[w, q], did(x, y, 2 * to + zl, c))
        ZWR[w, zh] = ZW[w, zh]

    def finish_grad(w, out):
        for q in (1, 3, 2):
            arrive(ZWR.at[w, (zh + 4 - q) % 4], vr.at[w, q])
        rows = ZWR[w].reshape(4 * UNITS, LANES)
        GOUT[w] = rows if w == 2 else rows.astype(F32).T.astype(BF16)
        leave(GOUT.at[w], out, 2 + w)

    send_tokens(0, tok)
    send_tokens(1, og)
    pack()
    send_weights(1)
    send_weights(3)
    weights_z(0)
    signs()
    tokens_z(0, 0)
    tokens_out(0, 0)
    tokens_z(1, 0)
    tokens_out(1, 0)
    tokens_z(0, 1)
    tokens_out(0, 1)
    tokens_z(1, 1)
    tokens_out(1, 1)
    send_weights(2)
    weights_z(1)
    weights_z(3)
    tokens_z(0, 2)
    tokens_out(0, 2)
    tokens_z(1, 2)
    tokens_out(1, 2)
    tokens_z(0, 3)
    tokens_out(0, 3)
    tokens_z(1, 3)
    tokens_out(1, 3)
    weights_z(2)
    tokens_y(0, (0,))
    tokens_y(0, (1,))
    tokens_y(0, (2,))
    tokens_y(0, (3,))
    rotate_in(0, y)
    rotate_in(0, ym)
    tokens_y(1, (0,))
    tokens_y(1, (1,))
    tokens_y(1, (2,))
    tokens_y(1, (3,))
    rotate_in(0, yp)
    to_core(0)
    to_core(1)
    to_core(2)
    to_core(3)
    tokens_far(0)
    weights_far()
    gates()
    rotate_weight(2)
    partial(0, 0)
    partial(0, 1)
    rotate_in(1, y)
    rotate_in(1, ym)
    rotate_in(1, yp)
    rotate_weight(0)
    rotate_weight(1)
    tokens_far(1)
    wgrads_other(2)
    hidden_grads()
    y_second(0, 0)
    y_second(0, 1)
    partial(1, 0)
    partial(1, 1)
    wgrads_own(2)
    x_first(2)
    turn(0)
    wgrads_other(0)
    wgrads_own(0)
    y_last(0)
    turn(1)
    wgrads_other(1)
    x_first(0)
    wgrads_own(1)
    x_first(1)
    z_second(0)
    y_second(1, 0)
    y_second(1, 1)
    x_last(2)
    x_last(0)
    y_last(1)
    x_last(1)
    finish_tokens(0, mixed)
    finish_grad(2, gd)
    z_second(1)
    finish_grad(0, gg)
    finish_grad(1, gu)
    finish_tokens(1, gtok)

    for cp in sent:
        cp.wait_send()
    for cp in leaving:
        cp.wait()

    @pl.when(home)
    def _():
        for cp in sent_home:
            cp.wait_send()

    @pl.when(away)
    def _():
        for cp in sent_away:
            cp.wait_send()


def copies(*refs):
    n = 5
    ins, outs, held, sems = refs[:n], refs[n:2 * n], refs[2 * n:3 * n], refs[3 * n]
    loads = [pltpu.make_async_copy(ins[i], held[i], sems.at[0, i]) for i in range(n)]
    stores = [pltpu.make_async_copy(held[i], outs[i], sems.at[1, i]) for i in range(n)]
    for cp in loads:
        cp.start()
    for i in range(n):
        loads[i].wait()
        stores[i].start()
    for cp in stores:
        cp.wait()


def shards(tokens, gate_weight, up_weight, down_weight, out_grad):
    dma = pltpu.SemaphoreType.DMA
    vm = pltpu.VMEM
    block = jax.ShapeDtypeStruct
    rows, cols = tokens.shape
    outs = (
        block((ROWS, LANES), F32), block((ROWS, LANES), F32),
        block((256, 256), BF16), block((256, 256), BF16), block((256, 256), BF16))
    results = pl.pallas_call(
        kernel,
        out_shape=outs,
        in_specs=[pl.BlockSpec(memory_space=pl.ANY)] * 5,
        out_specs=[pl.BlockSpec(memory_space=pltpu.HBM)] * 5,
        scratch_shapes=[
            vm((3, 256, 256), BF16),
            vm((2, ROWS, LANES), BF16),
            vm((2, 4, 8, ROWS, LANES), BF16),
            vm((4, 192, LANES), BF16),
            vm((4, 2, 4, 192, LANES), BF16),
            vm((LANES, LANES), BF16),
            vm((8, 256, LANES), F32),
            vm((3, 8, 256, LANES), BF16),
            vm((2, 8, 4, ROWS, LANES), BF16),
            vm((2, 4 * ROWS, 256), F32),
            vm((2, 4, 8, ROWS, LANES), BF16),
            vm((2, 8, ROWS, LANES), BF16),
            vm((2, 2, 8, ROWS, LANES), BF16),
            vm((2, 8, ROWS, LANES), BF16),
            vm((2, 5, ROWS, LANES), BF16),
            vm((2, 2, 2, ROWS, LANES), BF16),
            vm((2, 2, ROWS, LANES), BF16),
            vm((2, 2, 2, ROWS, LANES), BF16),
            vm((3, 4, 4, UNITS, LANES), F32),
            vm((3, 4, 4, UNITS, LANES), BF16),
            vm((3, 4, 4, UNITS, LANES), BF16),
            vm((3, 4, 4, UNITS, LANES), BF16),
            vm((3, 3, 4, UNITS, LANES), BF16),
            vm((3, 4, UNITS, LANES), BF16),
            vm((3, 4, UNITS, LANES), BF16),
            vm((3, 256, 4 * ROWS), BF16),
            dma((5,)), dma((2, 3)), dma((2, 8)), dma((2, 2)), dma((2, 4)), dma((2, 2)), dma((2, 2)),
            dma((4,)), dma((4,)),
            dma((2, 4, 2)), dma((2, 4, 2)), dma((2, 4)), dma((2, 4)),
            dma((4, 3)), dma((4, 3)),
            dma((8,)), dma((8,)), dma((2, 8)), dma((2, 8)), dma((2, 4)), dma((2, 4)),
            vm((2, ROWS, LANES), F32), vm((3, 256, 256), BF16), dma((5,)),
            dma((2, 9)), dma((2, 5)), dma((2, 2)), dma((2, 2)), dma((2, 2)), dma((2, 2)), dma((3, 3)), dma((3, 3)), dma((3, 4)), dma((3, 4)),
        ],
        compiler_params=pltpu.CompilerParams(
            collective_id=0, has_side_effects=True, vmem_limit_bytes=56 << 20),
        name="layer",
    )(tokens, out_grad, gate_weight, up_weight, down_weight)
    return pl.pallas_call(
        copies,
        out_shape=outs,
        in_specs=[pl.BlockSpec(memory_space=pltpu.HBM)] * 5,
        out_specs=[pl.BlockSpec(memory_space=pltpu.HBM)] * 5,
        scratch_shapes=[vm(o.shape, o.dtype) for o in outs] + [dma((2, 5))],
        compiler_params=pltpu.CompilerParams(vmem_limit_bytes=60 << 20),
        name="results",
    )(*results)


def solution(mesh):
    return jax.shard_map(
        shards,
        mesh=mesh,
        in_specs=(P("dp", "tensor"), P("tensor", "dp"), P("tensor", "dp"), P("dp", "tensor"), P("dp", "tensor")),
        out_specs=(P("dp", "tensor"), P("dp", "tensor"), P("tensor", "dp"), P("tensor", "dp"), P("dp", "tensor")),
        check_vma=False,
    )
```

```python
import math

import jax
import jax.numpy as jnp
from jax import lax
from jax.experimental import pallas as pl
from jax.experimental.pallas import tpu as pltpu
from jax.sharding import PartitionSpec as P

D = 2048
TOKENS = 2560
ROWS = 80
LANES = 256
UNITS = 64
MESH = pl.DeviceIdType.MESH
F32 = jnp.float32
BF16 = jnp.bfloat16


def dot_nn(a, b):
    return lax.dot_general(a, b, (((1,), (0,)), ((), ())), preferred_element_type=F32)


def dot_nt(a, b):
    return lax.dot_general(a, b, (((1,), (1,)), ((), ())), preferred_element_type=F32)


def butterflies(parts):
    parts = list(parts)
    for bit in range(3):
        step = 1 << bit
        for low in range(8):
            if not low & step:
                a, b = parts[low], parts[low | step]
                parts[low], parts[low | step] = a + b, a - b
    return parts


def kernel(tok_hbm, og_hbm, gw, uw, dw, mixed, gtok, gg, gu, gd,
           WIN, TIN, AB, PK, WB, H, FS, WR, ROT, GACT, MP, R1, R2, ZS, ZR, Q3, Q4, ZQ,
           WO, CS, CR, XS, X2, ZW, ZWR, GTT,
           loads, zs, zr, zfs, zfr, zes, zer, ws, wr, ys, yr, y2s, y2r, xs, xr, cs, cr, os_, or_, os2, or2,
           TOUT, GOUT, outs, es, er, q3s, q3r, q4s, q4r, gs, gr, vs, vr):
    dp = lax.axis_index("dp")
    te = lax.axis_index("tensor")
    x, zl, y = dp // 8, (dp // 4) % 2, dp % 4
    zh, c = te // 2, te % 2
    z = 2 * zh + zl
    k_own = te
    other = 1 - c
    home = c == zl
    xp, xm, xf = (x + 1) % 4, (x + 3) % 4, (x + 2) % 4
    yp, ym, yf = (y + 1) % 4, (y + 3) % 4, (y + 2) % 4

    def did(x_, y_, z_, c_):
        return ((x_ * 2 + z_ % 2) * 4 + y_, (z_ // 2) * 2 + c_)

    def rc(src, dst, send, recv, dev):
        return pltpu.make_async_remote_copy(
            src_ref=src, dst_ref=dst, send_sem=send, recv_sem=recv,
            device_id=dev, device_id_type=MESH)

    here = did(x, y, z, other)
    dev_x = (did(xp, y, z, c), did(xm, y, z, c), did(xf, y, z, c))
    dev_y = (did(x, yp, z, c), did(x, ym, z, c))
    sent, sent_home, sent_away = [], [], []

    def start(src, dst, send, recv, dev):
        cp = rc(src, dst, send, recv, dev)
        cp.start()
        sent.append(cp)

    leaving = []

    def leave(src, dst, n):
        cp = pltpu.make_async_copy(src, dst, outs.at[n])
        cp.start()
        leaving.append(cp)

    def arrive(dst, recv):
        rc(dst, dst, recv, recv, here).wait_recv()

    barrier = pltpu.get_barrier_semaphore()

    def greet(dev):
        pl.semaphore_signal(barrier, inc=1, device_id=dev, device_id_type=MESH)

    for dz in range(8):
        for cc in range(2):
            if dz or cc:
                greet(did(x, y, (z + dz) % 8, (c + cc) % 2))
    for dev in dev_x + dev_y:
        greet(dev)

    fetched = [pltpu.make_async_copy(ref, WIN.at[n], loads.at[n]) for n, ref in enumerate((gw, uw, dw))]
    fetched_tokens = [pltpu.make_async_copy(ref, TIN.at[n], loads.at[3 + n]) for n, ref in enumerate((tok_hbm, og_hbm))]
    for cp in fetched_tokens + fetched:
        cp.start()
    tok, og = TIN.at[0], TIN.at[1]

    for cp in fetched_tokens:
        cp.wait()
    pl.semaphore_wait(barrier, 20)

    def signs():
        i = lax.broadcasted_iota(jnp.int32, (LANES, LANES), 0)
        j = lax.broadcasted_iota(jnp.int32, (LANES, LANES), 1)
        b = i & j
        b = b ^ (b >> 4)
        b = b ^ (b >> 2)
        b = (b ^ (b >> 1)) & 1
        H[...] = (1 - 2 * b).astype(F32).astype(BF16)

    def pack():
        for cp in fetched:
            cp.wait()
        gwt = WIN[0].astype(F32).T.astype(BF16)
        uwt = WIN[1].astype(F32).T.astype(BF16)
        for q in range(4):
            PK[q, 0:UNITS] = gwt[q * UNITS:(q + 1) * UNITS]
            PK[q, UNITS:2 * UNITS] = uwt[q * UNITS:(q + 1) * UNITS]
            PK[q, 2 * UNITS:3 * UNITS] = WIN[2, q * UNITS:(q + 1) * UNITS, :]
        WB[x, c, zh] = PK[zh]

    dev_z = (did(x, y, (z + 1) % 8, c), did(x, y, (z + 7) % 8, c))
    own_z = (did(x, y, (z + 1) % 8, zl), did(x, y, (z + 7) % 8, zl))
    away = jnp.logical_not(home)

    def send_tokens(a, ref):
        for way in range(2):
            start(ref, AB.at[a, y, k_own], zs.at[a, way], zr.at[a, k_own], own_z[way])

        cp = rc(ref, AB.at[a, y, k_own], zs.at[a, 2], zr.at[a, k_own], here)

        @pl.when(home)
        def _():
            pltpu.make_async_copy(ref, AB.at[a, y, k_own], zs.at[a, 2]).start()

        @pl.when(away)
        def _():
            cp.start()
        sent_away.append(cp)

    def send_weights(q):
        to = (zh + q) % 4
        start(PK.at[to], WB.at[x, c, zh], ws.at[q], wr.at[q], did(x, y, 2 * to + zl, c))

    shift = zl
    at_home = [zh, (zh + 3) % 4, (zh + 1) % 4, (zh + 2) % 4]
    at_away = [(zh + 3 + shift) % 4, (zh + shift) % 4, (zh + 2 + shift) % 4, (zh + 1 + shift) % 4]
    step_zh = [jnp.where(home, p, q) for p, q in zip(at_home, at_away)]

    def pair(a, yy, pos):
        return AB.at[a, yy, pl.ds(2 * step_zh[pos], 2)]

    def tokens_z(a, pos):
        near = step_zh[pos]
        one = [AB.at[a, y, 2 * near + n] for n in range(2)]
        both = pair(a, y, pos)
        sem = [zr.at[a, 2 * near + n] for n in range(2)]

        def relay(way):
            return rc(both, both, zfs.at[a, way], zfr.at[a, near], dev_z[way])

        def last(way):
            return rc(one[way], one[way], zes.at[a, way], zer.at[a, way], dev_z[way])

        if 0 < pos < 3:
            from_home = relay(pos - 1)
            sent_home.append(from_home)
        from_away = relay(pos) if pos < 2 else last(pos - 2)
        sent_away.append(from_away)

        @pl.when(home)
        def _():
            if pos == 0:
                arrive(AB.at[a, y, 2 * near + other], zr.at[a, 2 * near + other])
                pltpu.make_async_copy((tok, og)[a], AB.at[a, y, k_own], zs.at[a, 2]).wait()
            elif pos < 3:
                arrive(both, zfr.at[a, near])
                from_home.start()
            else:
                arrive(one[0], zer.at[a, 0])
                arrive(one[1], zer.at[a, 1])

        @pl.when(away)
        def _():
            if pos < 2:
                arrive(one[0], sem[0])
                arrive(one[1], sem[1])
                from_away.start()
            else:
                arrive(both, zfr.at[a, near])
                from_away.start()

    def tokens_out(a, pos):
        for way in range(2):
            start(pair(a, y, pos), pair(a, y, pos), ys.at[a, pos, way], yr.at[a, pos, way], dev_y[way])

    def weights_z(q):
        frm = (zh + 4 - q) % 4
        if q:
            arrive(WB.at[x, c, frm], wr.at[q])
        for way in range(3):
            start(WB.at[x, c, frm], WB.at[x, c, frm], xs.at[q, way], xr.at[q, way], dev_x[way])

    def to_core(n):
        frm = (x, xm, xp, xf)[n]
        if n:
            for q in range(4):
                arrive(WB.at[frm, c, (zh + 4 - q) % 4], xr.at[q, n - 1])
        start(WB.at[frm, c], WB.at[frm, c], cs.at[n], cr.at[n], here)

    def tokens_y(a, steps=range(4)):
        for pos in steps:
            for way in range(2):
                frm = (ym, yp)[way]
                arrive(pair(a, frm, pos), yr.at[a, pos, way])
                if (pos < 2) == (way == 0):
                    start(pair(a, frm, pos), pair(a, frm, pos), y2s.at[a, pos], y2r.at[a, pos], dev_y[way])

    def weights_far():
        for n, frm in enumerate((x, xm, xp, xf)):
            arrive(WB.at[frm, other], cr.at[n])

    scale = 1.0 / math.sqrt(D)

    def spread(a, yy):
        def step(r, _):
            rows = pl.ds(pl.multiple_of(r * 16, 16), 16)
            parts = butterflies([FS[k, rows] for k in range(8)])
            for k in range(8):
                ROT[a, k, yy, rows] = (parts[k] * scale).astype(BF16)
            return 0
        lax.fori_loop(0, ROWS // 16, step, 0)

    def rotate_in(a, yy):
        FS[:, 0:ROWS] = dot_nn(AB[a, yy].reshape(8 * ROWS, LANES), H[...]).reshape(8, ROWS, LANES)
        spread(a, yy)

    def tokens_far(a):
        for pos in range(4):
            arrive(pair(a, yf, pos), y2r.at[a, pos])
        rotate_in(a, yf)


    def rot(a, k):
        return ROT[a, k].reshape(4 * ROWS, LANES)

    def weight(w, k):
        return jnp.concatenate(
            [WB[q, k % 2, k // 2, w * UNITS:(w + 1) * UNITS] for q in range(4)], axis=0)

    def rotate_weight(w):
        for k in range(8):
            FS[k] = dot_nn(weight(w, k), H[...])

        def step(r, _):
            rows = pl.ds(pl.multiple_of(r * 16, 16), 16)
            parts = butterflies([FS[k, rows] for k in range(8)])
            for k in range(8):
                WR[w, k, rows] = (parts[k] * scale).astype(BF16)
            return 0
        lax.fori_loop(0, 256 // 16, step, 0)

    def all_weight(w):
        return jnp.concatenate([weight(w, k) for k in range(8)], axis=1)

    def all_rot(a):
        return jnp.concatenate([rot(a, k) for k in range(8)], axis=1)

    kept = {}

    def gates():
        tokens = all_rot(0)
        gate = dot_nt(tokens, all_weight(0))
        up = dot_nt(tokens, all_weight(1))
        sigma = 1.0 / (1.0 + jnp.exp(-gate))
        hidden = gate * sigma * up
        kept[0] = hidden.astype(BF16)
        GTT[2] = hidden.T.astype(BF16)
        GACT[0] = up * sigma * (1.0 + gate * (1.0 - sigma))
        GACT[1] = gate * sigma

    def hidden_grads():
        grad_hidden = dot_nt(all_rot(1), all_weight(2))
        kept["gate"] = grad_hidden * GACT[0]
        kept["up"] = grad_hidden * GACT[1]
        kept[1] = jnp.concatenate([kept["gate"].astype(BF16), kept["up"].astype(BF16)], axis=1)

    def turn(w):
        GTT[w] = kept[("gate", "up")[w]].T.astype(BF16)

    def partial(a, h):
        for n in (2 * h, 2 * h + 1):
            for e in range(2):
                k = 2 * ((zh + n) % 4) + e
                matrix = jnp.concatenate([WR[0, k], WR[1, k]], axis=0) if a else WR[2, k]
                MP[a, :, k] = dot_nn(kept[a], matrix).astype(BF16).reshape(4, ROWS, LANES)
        y_first(a, h)

    def chunk(ref, n):
        return ref.at[pl.ds(2 * ((zh + n) % 4), 2)]

    def y_first(a, h):
        for n in (2 * h, 2 * h + 1):
            start(chunk(MP.at[a, yf], n), chunk(R1.at[a], n), os_.at[a, n], or_.at[a, n], dev_y[n % 2])
        for n in (2 * h, 2 * h + 1):
            frm = (ym, yp)[n % 2]
            start(chunk(MP.at[a, frm], n), chunk(R2.at[a, 1 - n % 2], n),
                  os_.at[a, 4 + n], or_.at[a, 4 + n], dev_y[1 - n % 2])

    def y_second(a, h):
        for n in (2 * h, 2 * h + 1):
            to = (yp, ym)[n % 2]
            arrive(chunk(R1.at[a], n), or_.at[a, n])
            ks = pl.ds(2 * ((zh + n) % 4), 2)
            MP[a, to, ks] = (MP[a, to, ks].astype(F32) + R1[a, ks].astype(F32)).astype(BF16)
            start(chunk(MP.at[a, to], n), chunk(R2.at[a, n % 2], n), os2.at[a, n], or2.at[a, n], dev_y[n % 2])

    def near_z(n):
        return did(x, y, (z + n) % 8, c)

    def owner(n, cc):
        return did(x, y, (z + n) % 8, cc)

    def to_zh(n):
        return (zh + n) % 4

    def y_last(a):
        for n in range(4):
            ks = pl.ds(2 * to_zh(n), 2)
            arrive(chunk(R2.at[a, 1 - n % 2], n), or_.at[a, 4 + n])
            arrive(chunk(R2.at[a, n % 2], n), or2.at[a, n])
            total = MP[a, y, ks].astype(F32) + R2[a, 0, ks].astype(F32) + R2[a, 1, ks].astype(F32)
            ZS[a, ks] = total.astype(BF16)
        far = [rc(ZS.at[a, 2 * to_zh(2) + w], Q4.at[a, w], q4s.at[a, w], q4r.at[a, w], near_z((2, 6)[w]))
               for w in range(2)]
        own = rc(ZS.at[a, 2 * zh + other], ZR.at[a, 0], es.at[a, 0], er.at[a, 0], here)
        thirds = [rc(ZS.at[a, pl.ds(2 * to_zh((1, 2)[w] + zl), 2)], Q3.at[a, w], q3s.at[a, w], q3r.at[a, w],
                     near_z((1, 7)[w])) for w in range(2)]
        firsts = [rc(ZS.at[a, 2 * to_zh((0, 3)[w] + zl) + cc], ZR.at[a, 1 + w], es.at[a, 1 + 2 * w + cc],
                     er.at[a, 1 + w], owner((1, 7)[w], cc)) for w in range(2) for cc in range(2)]
        sent_home.extend(far + [own])
        sent_away.extend(thirds + firsts)

        @pl.when(home)
        def _():
            for cp in far:
                cp.start()
            own.start()
            ZR[a, 0] = ZS[a, 2 * zh + c]

        @pl.when(away)
        def _():
            for cp in thirds + firsts:
                cp.start()

    def z_second(a):
        seconds = [rc(ZQ.at[a, w, cc], ZR.at[a, 3 + w], es.at[a, 5 + 2 * w + cc], er.at[a, 3 + w],
                      owner((2, 6)[w], cc)) for w in range(2) for cc in range(2)]
        sent_home.extend(seconds)

        @pl.when(home)
        def _():
            for w in range(2):
                arrive(Q3.at[a, w], q3r.at[a, w])
                arrive(Q4.at[a, w], q4r.at[a, w])
                for cc in range(2):
                    total = ZS[a, 2 * to_zh((1, 3)[w]) + cc].astype(F32) + Q3[a, w, cc].astype(F32)
                    if cc == w:
                        total = total + Q4[a, w].astype(F32)
                    ZQ[a, w, cc] = total.astype(BF16)
                    seconds[2 * w + cc].start()

    def finish_tokens(a, out):
        @pl.when(away)
        def _():
            arrive(ZR.at[a, 0], er.at[a, 0])
        total = ZR[a, 0].astype(F32)
        for n in range(1, 5):
            arrive(ZR.at[a, n], er.at[a, n])
            total = total + ZR[a, n].astype(F32)
        TOUT[a] = total
        leave(TOUT.at[a], out, a)

    def wgrads(w, parity, store):
        def step(q, _):
            g = dot_nn(GTT[w], ROT[w // 2, 2 * q + parity].reshape(4 * ROWS, LANES))
            for p in range(4):
                store(p, q, g[p * UNITS:(p + 1) * UNITS])
            return 0
        lax.fori_loop(0, 4, step, 0)

    def wgrads_other(w):
        def store(p, q, g):
            CS[w, p, q] = g.astype(BF16)
        wgrads(w, other, store)
        start(CS.at[w], CR.at[w], cs.at[4 + w], cr.at[4 + w], here)

    def wgrads_own(w):
        def store(p, q, g):
            WO[w, p, q] = g
        wgrads(w, c, store)

    def x_first(w):
        arrive(CR.at[w], cr.at[4 + w])
        for n, to in enumerate((xp, xm, xf)):
            XS[w, to] = (WO[w, to] + CR[w, to].astype(F32)).astype(BF16)
            start(XS.at[w, to], X2.at[w, n], gs.at[w, n], gr.at[w, n], dev_x[n])

    factor = 1.0 / math.sqrt(TOKENS)

    def x_last(w):
        total = WO[w, x] + CR[w, x].astype(F32)
        for n in range(3):
            arrive(X2.at[w, n], gr.at[w, n])
            total = total + X2[w, n].astype(F32)
        ZW[w] = (total * factor).astype(BF16)
        for q in (1, 3, 2):
            to = (zh + q) % 4
            start(ZW.at[w, to], ZWR.at[w, zh], vs.at[w, q], vr.at[w, q], did(x, y, 2 * to + zl, c))
        ZWR[w, zh] = ZW[w, zh]

    def finish_grad(w, out):
        for q in (1, 3, 2):
            arrive(ZWR.at[w, (zh + 4 - q) % 4], vr.at[w, q])
        rows = ZWR[w].reshape(4 * UNITS, LANES)
        GOUT[w] = rows if w == 2 else rows.astype(F32).T.astype(BF16)
        leave(GOUT.at[w], out, 2 + w)

    send_tokens(0, tok)
    send_tokens(1, og)
    pack()
    send_weights(1)
    send_weights(3)
    weights_z(0)
    signs()
    tokens_z(0, 0)
    tokens_out(0, 0)
    tokens_z(1, 0)
    tokens_out(1, 0)
    tokens_z(0, 1)
    tokens_out(0, 1)
    tokens_z(1, 1)
    tokens_out(1, 1)
    send_weights(2)
    weights_z(1)
    weights_z(3)
    tokens_z(0, 2)
    tokens_out(0, 2)
    tokens_z(1, 2)
    tokens_out(1, 2)
    tokens_z(0, 3)
    tokens_out(0, 3)
    tokens_z(1, 3)
    tokens_out(1, 3)
    weights_z(2)
    tokens_y(0, (0,))
    tokens_y(0, (1,))
    tokens_y(0, (2,))
    tokens_y(0, (3,))
    rotate_in(0, y)
    rotate_in(0, ym)
    tokens_y(1, (0,))
    tokens_y(1, (1,))
    tokens_y(1, (2,))
    tokens_y(1, (3,))
    rotate_in(0, yp)
    to_core(0)
    to_core(1)
    to_core(2)
    to_core(3)
    tokens_far(0)
    weights_far()
    gates()
    rotate_weight(2)
    partial(0, 0)
    partial(0, 1)
    rotate_in(1, y)
    rotate_in(1, ym)
    rotate_in(1, yp)
    rotate_weight(0)
    rotate_weight(1)
    tokens_far(1)
    wgrads_other(2)
    hidden_grads()
    y_second(0, 0)
    y_second(0, 1)
    partial(1, 0)
    partial(1, 1)
    early = len(sent)
    wgrads_own(2)
    x_first(2)
    turn(0)
    wgrads_other(0)
    wgrads_own(0)
    y_last(0)
    turn(1)
    wgrads_other(1)
    x_first(0)
    wgrads_own(1)
    x_first(1)
    z_second(0)
    y_second(1, 0)
    y_second(1, 1)
    x_last(2)
    x_last(0)
    for cp in sent[:early]:
        cp.wait_send()
    y_last(1)
    x_last(1)
    finish_tokens(0, mixed)
    finish_grad(2, gd)
    z_second(1)
    finish_grad(0, gg)
    finish_grad(1, gu)
    finish_tokens(1, gtok)

    for cp in sent[early:]:
        cp.wait_send()
    for cp in leaving:
        cp.wait()

    @pl.when(home)
    def _():
        for cp in sent_home:
            cp.wait_send()

    @pl.when(away)
    def _():
        for cp in sent_away:
            cp.wait_send()


def copies(*refs):
    n = 5
    ins, outs, held, sems = refs[:n], refs[n:2 * n], refs[2 * n:3 * n], refs[3 * n]
    loads = [pltpu.make_async_copy(ins[i], held[i], sems.at[0, i]) for i in range(n)]
    stores = [pltpu.make_async_copy(held[i], outs[i], sems.at[1, i]) for i in range(n)]
    for cp in loads:
        cp.start()
    for i in range(n):
        loads[i].wait()
        stores[i].start()
    for cp in stores:
        cp.wait()


def shards(tokens, gate_weight, up_weight, down_weight, out_grad):
    dma = pltpu.SemaphoreType.DMA
    vm = pltpu.VMEM
    block = jax.ShapeDtypeStruct
    rows, cols = tokens.shape
    outs = (
        block((ROWS, LANES), F32), block((ROWS, LANES), F32),
        block((256, 256), BF16), block((256, 256), BF16), block((256, 256), BF16))
    results = pl.pallas_call(
        kernel,
        out_shape=outs,
        in_specs=[pl.BlockSpec(memory_space=pl.ANY)] * 5,
        out_specs=[pl.BlockSpec(memory_space=pltpu.HBM)] * 5,
        scratch_shapes=[
            vm((3, 256, 256), BF16),
            vm((2, ROWS, LANES), BF16),
            vm((2, 4, 8, ROWS, LANES), BF16),
            vm((4, 192, LANES), BF16),
            vm((4, 2, 4, 192, LANES), BF16),
            vm((LANES, LANES), BF16),
            vm((8, 256, LANES), F32),
            vm((3, 8, 256, LANES), BF16),
            vm((2, 8, 4, ROWS, LANES), BF16),
            vm((2, 4 * ROWS, 256), F32),
            vm((2, 4, 8, ROWS, LANES), BF16),
            vm((2, 8, ROWS, LANES), BF16),
            vm((2, 2, 8, ROWS, LANES), BF16),
            vm((2, 8, ROWS, LANES), BF16),
            vm((2, 5, ROWS, LANES), BF16),
            vm((2, 2, 2, ROWS, LANES), BF16),
            vm((2, 2, ROWS, LANES), BF16),
            vm((2, 2, 2, ROWS, LANES), BF16),
            vm((3, 4, 4, UNITS, LANES), F32),
            vm((3, 4, 4, UNITS, LANES), BF16),
            vm((3, 4, 4, UNITS, LANES), BF16),
            vm((3, 4, 4, UNITS, LANES), BF16),
            vm((3, 3, 4, UNITS, LANES), BF16),
            vm((3, 4, UNITS, LANES), BF16),
            vm((3, 4, UNITS, LANES), BF16),
            vm((3, 256, 4 * ROWS), BF16),
            dma((5,)), dma((2, 3)), dma((2, 8)), dma((2, 2)), dma((2, 4)), dma((2, 2)), dma((2, 2)),
            dma((4,)), dma((4,)),
            dma((2, 4, 2)), dma((2, 4, 2)), dma((2, 4)), dma((2, 4)),
            dma((4, 3)), dma((4, 3)),
            dma((8,)), dma((8,)), dma((2, 8)), dma((2, 8)), dma((2, 4)), dma((2, 4)),
            vm((2, ROWS, LANES), F32), vm((3, 256, 256), BF16), dma((5,)),
            dma((2, 9)), dma((2, 5)), dma((2, 2)), dma((2, 2)), dma((2, 2)), dma((2, 2)), dma((3, 3)), dma((3, 3)), dma((3, 4)), dma((3, 4)),
        ],
        compiler_params=pltpu.CompilerParams(
            collective_id=0, has_side_effects=True, vmem_limit_bytes=56 << 20),
        name="layer",
    )(tokens, out_grad, gate_weight, up_weight, down_weight)
    return pl.pallas_call(
        copies,
        out_shape=outs,
        in_specs=[pl.BlockSpec(memory_space=pltpu.HBM)] * 5,
        out_specs=[pl.BlockSpec(memory_space=pltpu.HBM)] * 5,
        scratch_shapes=[vm(o.shape, o.dtype) for o in outs] + [dma((2, 5))],
        compiler_params=pltpu.CompilerParams(vmem_limit_bytes=60 << 20),
        name="results",
    )(*results)


def solution(mesh):
    return jax.shard_map(
        shards,
        mesh=mesh,
        in_specs=(P("dp", "tensor"), P("tensor", "dp"), P("tensor", "dp"), P("dp", "tensor"), P("dp", "tensor")),
        out_specs=(P("dp", "tensor"), P("dp", "tensor"), P("tensor", "dp"), P("tensor", "dp"), P("dp", "tensor")),
        check_vma=False,
    )
```

```python
import math

import jax
import jax.numpy as jnp
from jax import lax
from jax.experimental import pallas as pl
from jax.experimental.pallas import tpu as pltpu
from jax.sharding import PartitionSpec as P

D = 2048
TOKENS = 2560
ROWS = 80
LANES = 256
UNITS = 64
MESH = pl.DeviceIdType.MESH
F32 = jnp.float32
BF16 = jnp.bfloat16


def dot_nn(a, b):
    return lax.dot_general(a, b, (((1,), (0,)), ((), ())), preferred_element_type=F32)


def dot_nt(a, b):
    return lax.dot_general(a, b, (((1,), (1,)), ((), ())), preferred_element_type=F32)


def butterflies(parts):
    parts = list(parts)
    for bit in range(3):
        step = 1 << bit
        for low in range(8):
            if not low & step:
                a, b = parts[low], parts[low | step]
                parts[low], parts[low | step] = a + b, a - b
    return parts


def kernel(tok_hbm, og_hbm, gw, uw, dw, mixed, gtok, gg, gu, gd,
           WIN, TIN, AB, PK, WB, H, FS, WR, ROT, GACT, MP, R1, R2, ZS, ZR, Q3, Q4, ZQ,
           WO, CS, CR, XS, X2, ZW, ZWR, GTT,
           loads, zs, zr, zfs, zfr, zes, zer, ws, wr, ys, yr, y2s, y2r, xs, xr, cs, cr, os_, or_, os2, or2,
           TOUT, GOUT, outs, es, er, q3s, q3r, q4s, q4r, gs, gr, vs, vr):
    dp = lax.axis_index("dp")
    te = lax.axis_index("tensor")
    x, zl, y = dp // 8, (dp // 4) % 2, dp % 4
    zh, c = te // 2, te % 2
    z = 2 * zh + zl
    k_own = te
    other = 1 - c
    home = c == zl
    xp, xm, xf = (x + 1) % 4, (x + 3) % 4, (x + 2) % 4
    yp, ym, yf = (y + 1) % 4, (y + 3) % 4, (y + 2) % 4

    def did(x_, y_, z_, c_):
        return ((x_ * 2 + z_ % 2) * 4 + y_, (z_ // 2) * 2 + c_)

    def rc(src, dst, send, recv, dev):
        return pltpu.make_async_remote_copy(
            src_ref=src, dst_ref=dst, send_sem=send, recv_sem=recv,
            device_id=dev, device_id_type=MESH)

    here = did(x, y, z, other)
    dev_x = (did(xp, y, z, c), did(xm, y, z, c), did(xf, y, z, c))
    dev_y = (did(x, yp, z, c), did(x, ym, z, c))
    sent, sent_home, sent_away = [], [], []

    def start(src, dst, send, recv, dev):
        cp = rc(src, dst, send, recv, dev)
        cp.start()
        sent.append(cp)

    leaving = []

    def leave(src, dst, n):
        cp = pltpu.make_async_copy(src, dst, outs.at[n])
        cp.start()
        leaving.append(cp)

    def arrive(dst, recv):
        rc(dst, dst, recv, recv, here).wait_recv()

    barrier = pltpu.get_barrier_semaphore()

    def greet(dev):
        pl.semaphore_signal(barrier, inc=1, device_id=dev, device_id_type=MESH)

    for dz in range(8):
        for cc in range(2):
            if dz or cc:
                greet(did(x, y, (z + dz) % 8, (c + cc) % 2))
    for dev in dev_x + dev_y:
        greet(dev)

    fetched = [pltpu.make_async_copy(ref, WIN.at[n], loads.at[n]) for n, ref in enumerate((gw, uw, dw))]
    fetched_tokens = [pltpu.make_async_copy(ref, TIN.at[n], loads.at[3 + n]) for n, ref in enumerate((tok_hbm, og_hbm))]
    for cp in fetched_tokens + fetched:
        cp.start()
    tok, og = TIN.at[0], TIN.at[1]

    for cp in fetched_tokens:
        cp.wait()
    pl.semaphore_wait(barrier, 20)

    def signs():
        i = lax.broadcasted_iota(jnp.int32, (LANES, LANES), 0)
        j = lax.broadcasted_iota(jnp.int32, (LANES, LANES), 1)
        b = i & j
        b = b ^ (b >> 4)
        b = b ^ (b >> 2)
        b = (b ^ (b >> 1)) & 1
        H[...] = (1 - 2 * b).astype(F32).astype(BF16)

    def pack():
        for cp in fetched:
            cp.wait()
        gwt = WIN[0].astype(F32).T.astype(BF16)
        uwt = WIN[1].astype(F32).T.astype(BF16)
        for q in range(4):
            PK[q, 0:UNITS] = gwt[q * UNITS:(q + 1) * UNITS]
            PK[q, UNITS:2 * UNITS] = uwt[q * UNITS:(q + 1) * UNITS]
            PK[q, 2 * UNITS:3 * UNITS] = WIN[2, q * UNITS:(q + 1) * UNITS, :]
        WB[x, c, zh] = PK[zh]

    dev_z = (did(x, y, (z + 1) % 8, c), did(x, y, (z + 7) % 8, c))
    own_z = (did(x, y, (z + 1) % 8, zl), did(x, y, (z + 7) % 8, zl))
    away = jnp.logical_not(home)

    def send_tokens(a, ref):
        for way in range(2):
            start(ref, AB.at[a, y, k_own], zs.at[a, way], zr.at[a, k_own], own_z[way])

        cp = rc(ref, AB.at[a, y, k_own], zs.at[a, 2], zr.at[a, k_own], here)

        @pl.when(home)
        def _():
            pltpu.make_async_copy(ref, AB.at[a, y, k_own], zs.at[a, 2]).start()

        @pl.when(away)
        def _():
            cp.start()
        sent_away.append(cp)

    def send_weights(q):
        to = (zh + q) % 4
        start(PK.at[to], WB.at[x, c, zh], ws.at[q], wr.at[q], did(x, y, 2 * to + zl, c))

    shift = zl
    at_home = [zh, (zh + 3) % 4, (zh + 1) % 4, (zh + 2) % 4]
    at_away = [(zh + 3 + shift) % 4, (zh + shift) % 4, (zh + 2 + shift) % 4, (zh + 1 + shift) % 4]
    step_zh = [jnp.where(home, p, q) for p, q in zip(at_home, at_away)]

    def pair(a, yy, pos):
        return AB.at[a, yy, pl.ds(2 * step_zh[pos], 2)]

    def tokens_z(a, pos):
        near = step_zh[pos]
        one = [AB.at[a, y, 2 * near + n] for n in range(2)]
        both = pair(a, y, pos)
        sem = [zr.at[a, 2 * near + n] for n in range(2)]

        def relay(way):
            return rc(both, both, zfs.at[a, way], zfr.at[a, near], dev_z[way])

        def last(way):
            return rc(one[way], one[way], zes.at[a, way], zer.at[a, way], dev_z[way])

        if 0 < pos < 3:
            from_home = relay(pos - 1)
            sent_home.append(from_home)
        from_away = relay(pos) if pos < 2 else last(pos - 2)
        sent_away.append(from_away)

        @pl.when(home)
        def _():
            if pos == 0:
                arrive(AB.at[a, y, 2 * near + other], zr.at[a, 2 * near + other])
                pltpu.make_async_copy((tok, og)[a], AB.at[a, y, k_own], zs.at[a, 2]).wait()
            elif pos < 3:
                arrive(both, zfr.at[a, near])
                from_home.start()
            else:
                arrive(one[0], zer.at[a, 0])
                arrive(one[1], zer.at[a, 1])

        @pl.when(away)
        def _():
            if pos < 2:
                arrive(one[0], sem[0])
                arrive(one[1], sem[1])
                from_away.start()
            else:
                arrive(both, zfr.at[a, near])
                from_away.start()

    def tokens_out(a, pos):
        for way in range(2):
            start(pair(a, y, pos), pair(a, y, pos), ys.at[a, pos, way], yr.at[a, pos, way], dev_y[way])

    def weights_z(q):
        frm = (zh + 4 - q) % 4
        if q:
            arrive(WB.at[x, c, frm], wr.at[q])
        for way in range(3):
            start(WB.at[x, c, frm], WB.at[x, c, frm], xs.at[q, way], xr.at[q, way], dev_x[way])

    def to_core(n):
        frm = (x, xm, xp, xf)[n]
        if n:
            for q in range(4):
                arrive(WB.at[frm, c, (zh + 4 - q) % 4], xr.at[q, n - 1])
        start(WB.at[frm, c], WB.at[frm, c], cs.at[n], cr.at[n], here)

    def tokens_y(a, steps=range(4)):
        for pos in steps:
            for way in range(2):
                frm = (ym, yp)[way]
                arrive(pair(a, frm, pos), yr.at[a, pos, way])
                if (pos < 2) == (way == 0):
                    start(pair(a, frm, pos), pair(a, frm, pos), y2s.at[a, pos], y2r.at[a, pos], dev_y[way])

    def weights_far():
        for n, frm in enumerate((x, xm, xp, xf)):
            arrive(WB.at[frm, other], cr.at[n])

    scale = 1.0 / math.sqrt(D)

    def spread(a, yy):
        def step(r, _):
            rows = pl.ds(pl.multiple_of(r * 16, 16), 16)
            parts = butterflies([FS[k, rows] for k in range(8)])
            for k in range(8):
                ROT[a, k, yy, rows] = (parts[k] * scale).astype(BF16)
            return 0
        lax.fori_loop(0, ROWS // 16, step, 0)

    def rotate_in(a, yy):
        FS[:, 0:ROWS] = dot_nn(AB[a, yy].reshape(8 * ROWS, LANES), H[...]).reshape(8, ROWS, LANES)
        spread(a, yy)

    def tokens_far(a):
        for pos in range(4):
            arrive(pair(a, yf, pos), y2r.at[a, pos])
        rotate_in(a, yf)


    def rot(a, k):
        return ROT[a, k].reshape(4 * ROWS, LANES)

    def weight(w, k):
        return jnp.concatenate(
            [WB[q, k % 2, k // 2, w * UNITS:(w + 1) * UNITS] for q in range(4)], axis=0)

    def rotate_weight(w):
        for k in range(8):
            FS[k] = dot_nn(weight(w, k), H[...])

        def step(r, _):
            rows = pl.ds(pl.multiple_of(r * 16, 16), 16)
            parts = butterflies([FS[k, rows] for k in range(8)])
            for k in range(8):
                WR[w, k, rows] = (parts[k] * scale).astype(BF16)
            return 0
        lax.fori_loop(0, 256 // 16, step, 0)

    def all_weight(w):
        return jnp.concatenate([weight(w, k) for k in range(8)], axis=1)

    def all_rot(a):
        return jnp.concatenate([rot(a, k) for k in range(8)], axis=1)

    kept = {}

    def gates():
        tokens = all_rot(0)
        gate = dot_nt(tokens, all_weight(0))
        up = dot_nt(tokens, all_weight(1))
        sigma = 1.0 / (1.0 + jnp.exp(-gate))
        hidden = gate * sigma * up
        kept[0] = hidden.astype(BF16)
        GTT[2] = hidden.T.astype(BF16)
        GACT[0] = up * sigma * (1.0 + gate * (1.0 - sigma))
        GACT[1] = gate * sigma

    def hidden_grads():
        grad_hidden = dot_nt(all_rot(1), all_weight(2))
        kept["gate"] = grad_hidden * GACT[0]
        kept["up"] = grad_hidden * GACT[1]
        kept[1] = jnp.concatenate([kept["gate"].astype(BF16), kept["up"].astype(BF16)], axis=1)

    def turn(w):
        GTT[w] = kept[("gate", "up")[w]].T.astype(BF16)

    def partial(a, h):
        for n in (2 * h, 2 * h + 1):
            for e in range(2):
                k = 2 * ((zh + n) % 4) + e
                matrix = jnp.concatenate([WR[0, k], WR[1, k]], axis=0) if a else WR[2, k]
                MP[a, :, k] = dot_nn(kept[a], matrix).astype(BF16).reshape(4, ROWS, LANES)
        y_first(a, h)

    def chunk(ref, n):
        return ref.at[pl.ds(2 * ((zh + n) % 4), 2)]

    def y_first(a, h):
        for n in (2 * h, 2 * h + 1):
            start(chunk(MP.at[a, yf], n), chunk(R1.at[a], n), os_.at[a, n], or_.at[a, n], dev_y[n % 2])
        for n in (2 * h, 2 * h + 1):
            frm = (ym, yp)[n % 2]
            start(chunk(MP.at[a, frm], n), chunk(R2.at[a, 1 - n % 2], n),
                  os_.at[a, 4 + n], or_.at[a, 4 + n], dev_y[1 - n % 2])

    def y_second(a, h):
        for n in (2 * h, 2 * h + 1):
            to = (yp, ym)[n % 2]
            arrive(chunk(R1.at[a], n), or_.at[a, n])
            ks = pl.ds(2 * ((zh + n) % 4), 2)
            MP[a, to, ks] = (MP[a, to, ks].astype(F32) + R1[a, ks].astype(F32)).astype(BF16)
            start(chunk(MP.at[a, to], n), chunk(R2.at[a, n % 2], n), os2.at[a, n], or2.at[a, n], dev_y[n % 2])

    def near_z(n):
        return did(x, y, (z + n) % 8, c)

    def owner(n, cc):
        return did(x, y, (z + n) % 8, cc)

    def to_zh(n):
        return (zh + n) % 4

    def y_last(a):
        for n in range(4):
            ks = pl.ds(2 * to_zh(n), 2)
            arrive(chunk(R2.at[a, 1 - n % 2], n), or_.at[a, 4 + n])
            arrive(chunk(R2.at[a, n % 2], n), or2.at[a, n])
            total = MP[a, y, ks].astype(F32) + R2[a, 0, ks].astype(F32) + R2[a, 1, ks].astype(F32)
            ZS[a, ks] = total.astype(BF16)
        far = [rc(ZS.at[a, 2 * to_zh(2) + w], Q4.at[a, w], q4s.at[a, w], q4r.at[a, w], near_z((2, 6)[w]))
               for w in range(2)]
        own = rc(ZS.at[a, 2 * zh + other], ZR.at[a, 0], es.at[a, 0], er.at[a, 0], here)
        thirds = [rc(ZS.at[a, pl.ds(2 * to_zh((1, 2)[w] + zl), 2)], Q3.at[a, w], q3s.at[a, w], q3r.at[a, w],
                     near_z((1, 7)[w])) for w in range(2)]
        firsts = [rc(ZS.at[a, 2 * to_zh((0, 3)[w] + zl) + cc], ZR.at[a, 1 + w], es.at[a, 1 + 2 * w + cc],
                     er.at[a, 1 + w], owner((1, 7)[w], cc)) for w in range(2) for cc in range(2)]
        sent_home.extend(far + [own])
        sent_away.extend(thirds + firsts)

        @pl.when(home)
        def _():
            for cp in far:
                cp.start()
            own.start()
            ZR[a, 0] = ZS[a, 2 * zh + c]

        @pl.when(away)
        def _():
            for cp in thirds + firsts:
                cp.start()

    def z_second(a):
        seconds = [rc(ZQ.at[a, w, cc], ZR.at[a, 3 + w], es.at[a, 5 + 2 * w + cc], er.at[a, 3 + w],
                      owner((2, 6)[w], cc)) for w in range(2) for cc in range(2)]
        sent_home.extend(seconds)

        @pl.when(home)
        def _():
            for w in range(2):
                arrive(Q3.at[a, w], q3r.at[a, w])
                arrive(Q4.at[a, w], q4r.at[a, w])
                for cc in range(2):
                    total = ZS[a, 2 * to_zh((1, 3)[w]) + cc].astype(F32) + Q3[a, w, cc].astype(F32)
                    if cc == w:
                        total = total + Q4[a, w].astype(F32)
                    ZQ[a, w, cc] = total.astype(BF16)
                    seconds[2 * w + cc].start()

    def finish_tokens(a, out):
        @pl.when(away)
        def _():
            arrive(ZR.at[a, 0], er.at[a, 0])
        total = ZR[a, 0].astype(F32)
        for n in range(1, 5):
            arrive(ZR.at[a, n], er.at[a, n])
            total = total + ZR[a, n].astype(F32)
        TOUT[a] = total
        leave(TOUT.at[a], out, a)

    def wgrads(w, parity, store):
        def step(q, _):
            g = dot_nn(GTT[w], ROT[w // 2, 2 * q + parity].reshape(4 * ROWS, LANES))
            for p in range(4):
                store(p, q, g[p * UNITS:(p + 1) * UNITS])
            return 0
        lax.fori_loop(0, 4, step, 0)

    def wgrads_other(w):
        def store(p, q, g):
            CS[w, p, q] = g.astype(BF16)
        wgrads(w, other, store)
        start(CS.at[w], CR.at[w], cs.at[4 + w], cr.at[4 + w], here)

    def wgrads_own(w):
        def store(p, q, g):
            WO[w, p, q] = g
        wgrads(w, c, store)

    def x_first(w):
        arrive(CR.at[w], cr.at[4 + w])
        for n, to in enumerate((xp, xm, xf)):
            XS[w, to] = (WO[w, to] + CR[w, to].astype(F32)).astype(BF16)
            start(XS.at[w, to], X2.at[w, n], gs.at[w, n], gr.at[w, n], dev_x[n])

    factor = 1.0 / math.sqrt(TOKENS)

    def x_last(w):
        total = WO[w, x] + CR[w, x].astype(F32)
        for n in range(3):
            arrive(X2.at[w, n], gr.at[w, n])
            total = total + X2[w, n].astype(F32)
        ZW[w] = (total * factor).astype(BF16)
        for q in (1, 3, 2):
            to = (zh + q) % 4
            start(ZW.at[w, to], ZWR.at[w, zh], vs.at[w, q], vr.at[w, q], did(x, y, 2 * to + zl, c))
        ZWR[w, zh] = ZW[w, zh]

    def finish_grad(w, out):
        for q in (1, 3, 2):
            arrive(ZWR.at[w, (zh + 4 - q) % 4], vr.at[w, q])
        rows = ZWR[w].reshape(4 * UNITS, LANES)
        GOUT[w] = rows if w == 2 else rows.astype(F32).T.astype(BF16)
        leave(GOUT.at[w], out, 2 + w)

    send_tokens(0, tok)
    send_tokens(1, og)
    pack()
    send_weights(1)
    send_weights(3)
    weights_z(0)
    signs()
    tokens_z(0, 0)
    tokens_out(0, 0)
    tokens_z(1, 0)
    tokens_out(1, 0)
    tokens_z(0, 1)
    tokens_out(0, 1)
    tokens_z(1, 1)
    tokens_out(1, 1)
    send_weights(2)
    weights_z(1)
    weights_z(3)
    tokens_z(0, 2)
    tokens_out(0, 2)
    tokens_z(1, 2)
    tokens_out(1, 2)
    tokens_z(0, 3)
    tokens_out(0, 3)
    tokens_z(1, 3)
    tokens_out(1, 3)
    weights_z(2)
    tokens_y(0, (0,))
    tokens_y(0, (1,))
    tokens_y(0, (2,))
    tokens_y(0, (3,))
    rotate_in(0, y)
    rotate_in(0, ym)
    tokens_y(1, (0,))
    tokens_y(1, (1,))
    tokens_y(1, (2,))
    tokens_y(1, (3,))
    rotate_in(0, yp)
    to_core(0)
    to_core(1)
    to_core(2)
    to_core(3)
    tokens_far(0)
    weights_far()
    gates()
    rotate_weight(2)
    partial(0, 0)
    partial(0, 1)
    rotate_in(1, y)
    rotate_in(1, ym)
    rotate_in(1, yp)
    rotate_weight(0)
    rotate_weight(1)
    tokens_far(1)
    wgrads_other(2)
    hidden_grads()
    y_second(0, 0)
    y_second(0, 1)
    partial(1, 0)
    partial(1, 1)
    early = len(sent)
    wgrads_own(2)
    x_first(2)
    turn(0)
    wgrads_other(0)
    wgrads_own(0)
    y_last(0)
    turn(1)
    wgrads_other(1)
    x_first(0)
    wgrads_own(1)
    x_first(1)
    z_second(0)
    y_second(1, 0)
    y_second(1, 1)
    x_last(2)
    x_last(0)
    for cp in sent[:early]:
        cp.wait_send()
    later = len(sent)
    y_last(1)
    x_last(1)
    finish_tokens(0, mixed)
    finish_grad(2, gd)
    z_second(1)
    finish_grad(0, gg)
    finish_grad(1, gu)
    for cp in sent[early:later]:
        cp.wait_send()
    finish_tokens(1, gtok)

    for cp in sent[later:]:
        cp.wait_send()
    for cp in leaving:
        cp.wait()

    @pl.when(home)
    def _():
        for cp in sent_home:
            cp.wait_send()

    @pl.when(away)
    def _():
        for cp in sent_away:
            cp.wait_send()


def copies(*refs):
    n = 5
    ins, outs, held, sems = refs[:n], refs[n:2 * n], refs[2 * n:3 * n], refs[3 * n]
    loads = [pltpu.make_async_copy(ins[i], held[i], sems.at[0, i]) for i in range(n)]
    stores = [pltpu.make_async_copy(held[i], outs[i], sems.at[1, i]) for i in range(n)]
    for cp in loads:
        cp.start()
    for i in range(n):
        loads[i].wait()
        stores[i].start()
    for cp in stores:
        cp.wait()


def shards(tokens, gate_weight, up_weight, down_weight, out_grad):
    dma = pltpu.SemaphoreType.DMA
    vm = pltpu.VMEM
    block = jax.ShapeDtypeStruct
    rows, cols = tokens.shape
    outs = (
        block((ROWS, LANES), F32), block((ROWS, LANES), F32),
        block((256, 256), BF16), block((256, 256), BF16), block((256, 256), BF16))
    results = pl.pallas_call(
        kernel,
        out_shape=outs,
        in_specs=[pl.BlockSpec(memory_space=pl.ANY)] * 5,
        out_specs=[pl.BlockSpec(memory_space=pltpu.HBM)] * 5,
        scratch_shapes=[
            vm((3, 256, 256), BF16),
            vm((2, ROWS, LANES), BF16),
            vm((2, 4, 8, ROWS, LANES), BF16),
            vm((4, 192, LANES), BF16),
            vm((4, 2, 4, 192, LANES), BF16),
            vm((LANES, LANES), BF16),
            vm((8, 256, LANES), F32),
            vm((3, 8, 256, LANES), BF16),
            vm((2, 8, 4, ROWS, LANES), BF16),
            vm((2, 4 * ROWS, 256), F32),
            vm((2, 4, 8, ROWS, LANES), BF16),
            vm((2, 8, ROWS, LANES), BF16),
            vm((2, 2, 8, ROWS, LANES), BF16),
            vm((2, 8, ROWS, LANES), BF16),
            vm((2, 5, ROWS, LANES), BF16),
            vm((2, 2, 2, ROWS, LANES), BF16),
            vm((2, 2, ROWS, LANES), BF16),
            vm((2, 2, 2, ROWS, LANES), BF16),
            vm((3, 4, 4, UNITS, LANES), F32),
            vm((3, 4, 4, UNITS, LANES), BF16),
            vm((3, 4, 4, UNITS, LANES), BF16),
            vm((3, 4, 4, UNITS, LANES), BF16),
            vm((3, 3, 4, UNITS, LANES), BF16),
            vm((3, 4, UNITS, LANES), BF16),
            vm((3, 4, UNITS, LANES), BF16),
            vm((3, 256, 4 * ROWS), BF16),
            dma((5,)), dma((2, 3)), dma((2, 8)), dma((2, 2)), dma((2, 4)), dma((2, 2)), dma((2, 2)),
            dma((4,)), dma((4,)),
            dma((2, 4, 2)), dma((2, 4, 2)), dma((2, 4)), dma((2, 4)),
            dma((4, 3)), dma((4, 3)),
            dma((8,)), dma((8,)), dma((2, 8)), dma((2, 8)), dma((2, 4)), dma((2, 4)),
            vm((2, ROWS, LANES), F32), vm((3, 256, 256), BF16), dma((5,)),
            dma((2, 9)), dma((2, 5)), dma((2, 2)), dma((2, 2)), dma((2, 2)), dma((2, 2)), dma((3, 3)), dma((3, 3)), dma((3, 4)), dma((3, 4)),
        ],
        compiler_params=pltpu.CompilerParams(
            collective_id=0, has_side_effects=True, vmem_limit_bytes=56 << 20),
        name="layer",
    )(tokens, out_grad, gate_weight, up_weight, down_weight)
    return pl.pallas_call(
        copies,
        out_shape=outs,
        in_specs=[pl.BlockSpec(memory_space=pltpu.HBM)] * 5,
        out_specs=[pl.BlockSpec(memory_space=pltpu.HBM)] * 5,
        scratch_shapes=[vm(o.shape, o.dtype) for o in outs] + [dma((2, 5))],
        compiler_params=pltpu.CompilerParams(vmem_limit_bytes=60 << 20),
        name="results",
    )(*results)


def solution(mesh):
    return jax.shard_map(
        shards,
        mesh=mesh,
        in_specs=(P("dp", "tensor"), P("tensor", "dp"), P("tensor", "dp"), P("dp", "tensor"), P("dp", "tensor")),
        out_specs=(P("dp", "tensor"), P("dp", "tensor"), P("tensor", "dp"), P("tensor", "dp"), P("dp", "tensor")),
        check_vma=False,
    )
```
